128 devices in a mesh: gx: 16 (over z_hi, x, core), gy: 8 (over y, z_lo).
Axes of the slice: x: 4, y: 4, z: 4 (z_hi: 2, z_lo: 2; z = z_hi * 2 + z_lo), core: 2. Of those that a mesh axis runs over, the one named last changes fastest.
Arguments:
- populations: float32 [19, 64, 256, 128], P(None, 'gx', 'gy'), may hold values from 0.02 to 0.09
- marker_weights: bfloat16 [6144, 64, 128], P(('gx', 'gy')), may hold values from 0 to 0.03125
- marker_force: bfloat16 [6144, 3, 128], P(('gx', 'gy')), may hold values from -0.59765625 to 0.59765625
- owner_device: int32 [6144, 1], P(('gx', 'gy')), may hold values from 0 to 127; in each aligned block of 48 rows (0 to 47, 48 to 95, ...) at most 2 rows name the same one
- stencil_base: int32 [6144, 3], P(('gx', 'gy')), may hold values from 0 to 124, as said below
- block_swimmer: int32 [6144], P(('gx', 'gy')), may hold values from 0 to 511, as said below
Outputs:
- new_populations: float32 [19, 64, 256, 128], P(None, 'gx', 'gy')
- marker_velocity: float32 [6144, 3, 128], P(('gx', 'gy'))
- swimmer_velocity: float32 [3, 512], P(None, ('gx', 'gy'))
The draws below stay inside these ranges and needn't reach their ends.
Inputs may be any that keep to these rules, and one draw needn't show every extreme that they name: `owner_device`: among the blocks held by one device (aligned runs of 48 rows), no device is named more than 2 times, and some device is named exactly 2 times. `stencil_base`: component 0 lies in 0 to 0, component 1 in 0 to 28, component 2 in 0 to 124; each bound is taken by some block. `block_swimmer`: the blocks held by device d (gx slowest) belong to swimmers d * 4 to d * 4 + 3, and every swimmer has a block.
All inputs are finite; a program needn't handle non-finite values.
Results may differ from the reference program's by a relative error of at most 0.00056.
Values may be sent and summed in bfloat16 or wider, within the bound.
A program may use at most 64 MiB of HBM per device.

```python
import math
import jax
import jax.numpy as jnp
import numpy as np
from jax import lax

CX = 4
CY = 32
NZ = 128
STEN = 4
MARK = 128
BLK_DEV = 48
SWIM_DEV = 4
NX = 64
NY = 256
BLOCKS = 6144
SWIMMERS = 512
CAP = 2
N_GY = 8
DEVICES = 128


def draw_stencil_base(key, part):
    key_slab, key_strip, key_column = jax.random.split(jax.random.fold_in(key, 11), 3)
    along_slab = jax.random.randint(key_slab, (BLOCKS,), 0, CX - 3, dtype=jnp.int32).at[0].set(CX - 4)
    along_strip = jax.random.randint(key_strip, (BLOCKS,), 0, CY - 3, dtype=jnp.int32).at[0].set(CY - 4)
    along_column = jax.random.randint(key_column, (BLOCKS,), 0, NZ - 3, dtype=jnp.int32).at[0].set(NZ - 4)
    return jnp.stack([along_slab, along_strip, along_column], axis=1)


def draw_block_swimmer(key, part):
    block_rows = jnp.arange(BLOCKS, dtype=jnp.int32)
    device_rank = block_rows // BLK_DEV
    within = block_rows % BLK_DEV
    random_slot = jax.random.randint(jax.random.fold_in(key, 7), (BLOCKS,), 0, SWIM_DEV, dtype=jnp.int32)
    return device_rank * SWIM_DEV + jnp.where(within < SWIM_DEV, within, random_slot)


def block_scale(rng, shape, pieces, least, largest):
    level, own = 1.0, jax.random.fold_in(rng, 6)
    for position, blocks in pieces:
        steps = jnp.exp(jax.random.uniform(jax.random.fold_in(own, position), (blocks,), jnp.float32, least / len(pieces), largest / len(pieces)))
        level = level * jnp.repeat(steps, shape[position] // blocks).reshape([-1 if axis == position else 1 for axis in range(len(shape))])
    return level


def deal_out(rng, own, number, rows, number_of, top, bound, slope):
    ranking = jax.random.permutation(rng, number_of)
    crowded, common = load_shares(number_of, rows * top, bound, slope, True), load_shares(number_of, rows * top, bound, slope, False)
    places = jnp.arange(number_of)

    def named(lengths, offset_by):
        used = int((lengths > 0).sum())
        fixed = max(1, used // 4)
        shifted = fixed + (places - fixed + offset_by * (used - fixed)) % max(1, number_of - fixed)
        return jnp.zeros((number_of,), jnp.int32).at[ranking[jnp.where(places < fixed, places, shifted)]].set(jnp.asarray(lengths, jnp.int32))

    lengths = jnp.where(number % 4 == 0, named(crowded, number // 4), named(common, number - number // 4 - 1))
    mixed = jax.random.permutation(jax.random.fold_in(own, 3), number_of)
    donor, sink = mixed[0:number_of // 2 * 2:2], mixed[1:number_of // 2 * 2:2]
    margin = jnp.minimum(lengths[donor] - 1, bound - lengths[sink]) // 2
    margin = jnp.where((donor == ranking[0]) | (sink == ranking[0]) | (lengths[sink] == 0), 0, jnp.maximum(margin, 0))
    shifted = jax.random.randint(jax.random.fold_in(own, 4), (number_of // 2,), 0, 1 << 20) % (margin + 1)
    lengths = lengths.at[donor].add(-shifted).at[sink].add(shifted)
    items = jnp.searchsorted(jnp.cumsum(lengths), jnp.arange(rows * top), side="right").astype(jnp.int32)
    grid = items.reshape(top, rows).T
    grid = grid[jax.random.permutation(jax.random.fold_in(own, 1), rows)]
    offset_by = jax.random.randint(jax.random.fold_in(own, 2), (rows, 1), 0, top)
    return jnp.take_along_axis(grid, (jnp.arange(top)[None, :] + offset_by) % top, axis=1)


def load_shares(count, total, most, lean, full):
    weights = [(1 << 20) // math.isqrt(grade ** lean) + 1 for grade in range(1, count + 1)]
    largest = most if full else min(most, max(-(-total // count), total * weights[0] // sum(weights)))
    least = 1 if total - largest >= count - 1 else 0
    given, spare = [largest] + [least] * (count - 1), total - largest - least * (count - 1)
    while spare > 0:
        movable = [i for i in range(1, count) if given[i] < largest] or [i for i in range(1, count) if given[i] < most]
        pool, remaining = sum([weights[i] for i in movable]), spare
        for i in movable:
            addition = min(most - given[i], max(1, remaining * weights[i] // pool), spare)
            given[i] = given[i] + addition
            spare = spare - addition
    return np.array(given)


def gaussian(stream_key, dims, spread, most, cuts=(), kind=jnp.bfloat16):
    values = jax.random.normal(stream_key, dims, jnp.float32) * spread
    if len(cuts) > 0:
        values = block_scale(stream_key, dims, cuts, -0.22, 0.18) * values
    return jnp.clip(values, min=-most, max=most).astype(kind)


def setup_inputs(seed: int = 0) -> dict:
    keys = jax.random.split(jax.random.key(seed), 7)
    populations = jnp.clip(0.02 + 0.07000000402331352 * jax.random.uniform(keys[0], (19, NX, NY, NZ), jnp.float32) ** block_scale(keys[0], (19, NX, NY, NZ), ((1, 16), (2, 8)), -0.2, 0.2), 0.02, 0.09)
    marker_weights = jnp.clip(0.03125 * jax.random.uniform(keys[1], (BLOCKS, STEN * STEN * STEN, MARK), jnp.float32) ** block_scale(keys[1], (BLOCKS, STEN * STEN * STEN, MARK), ((0, 128),), -0.2, 0.2), 0.0, 0.03125).astype(jnp.bfloat16)
    marker_force = gaussian(keys[2], (BLOCKS, 3, MARK), 0.1, 0.59765625, ((0, 128),))
    owner_device_keys = jax.random.split(jax.random.fold_in(keys[3], 1), BLOCKS // BLK_DEV)
    owner_device_turns = jax.random.permutation(jax.random.fold_in(keys[3], 3), BLOCKS // BLK_DEV)
    owner_device = jax.vmap(lambda own, number: deal_out(jax.random.fold_in(keys[3], 2), own, number, BLK_DEV, DEVICES, 1, CAP, 2))(owner_device_keys, owner_device_turns).reshape((BLOCKS, 1))
    stencil_base = draw_stencil_base(jax.random.fold_in(keys[6], 71), 0)
    block_swimmer = draw_block_swimmer(jax.random.fold_in(keys[6], 71), 0)
    return {"populations": populations, "marker_weights": marker_weights, "marker_force": marker_force, "owner_device": owner_device, "stencil_base": stencil_base, "block_swimmer": block_swimmer}


velocities = np.array([[0, 0, 0], [1, 0, 0], [-1, 0, 0], [0, 1, 0], [0, -1, 0], [0, 0, 1], [0, 0, -1], [1, 1, 0], [-1, -1, 0], [1, -1, 0], [-1, 1, 0], [1, 0, 1], [-1, 0, -1], [1, 0, -1], [-1, 0, 1], [0, 1, 1], [0, -1, -1], [0, 1, -1], [0, -1, 1]])
opposite = [0, 2, 1, 4, 3, 6, 5, 8, 7, 10, 9, 12, 11, 14, 13, 16, 15, 18, 17]
lattice_weights = np.array([1.0 / 3.0] + [1.0 / 18.0] * 6 + [1.0 / 36.0] * 12)
relax_time = 0.8
speed_scale = 20.0


def signed_total(stack, component):
    plus_list = [i for i in range(19) if velocities[i, component] == 1]
    minus_list = [i for i in range(19) if velocities[i, component] == -1]
    return jnp.sum(stack[np.array(plus_list)], axis=0) - jnp.sum(stack[np.array(minus_list)], axis=0)


def moments(fields):
    density = jnp.sum(fields, axis=0)
    momentum = jnp.stack([signed_total(fields, k) for k in range(3)])
    return density, momentum


def collide(fields, forcing):
    density, momentum = moments(fields)
    velocity = (momentum + relax_time * forcing) / density
    project_list = []
    for direction in range(19):
        term = jnp.zeros_like(density)
        for k in range(3):
            sign = int(velocities[direction, k])
            if sign == 1:
                term = term + velocity[k]
            elif sign == -1:
                term = term - velocity[k]
        project_list.append(term)
    project = jnp.stack(project_list)
    square = jnp.sum(velocity * velocity, axis=0)
    weights = jnp.asarray(lattice_weights, jnp.float32)[:, None, None, None]
    equilibrium = weights * density * (1.0 + 3.0 * project + 4.5 * project * project - 1.5 * square)
    return fields - (fields - equilibrium) / relax_time


def stream(padded, first_row, total_rows):
    slab_cells = padded.shape[1] - 2
    strip_cells = padded.shape[2] - 2
    height = padded.shape[3]
    global_rows = first_row + jnp.arange(strip_cells, dtype=jnp.int32)
    column_cells = jnp.arange(height, dtype=jnp.int32)
    result = []
    for direction in range(19):
        move_east = int(velocities[direction, 0])
        move_north = int(velocities[direction, 1])
        move_up = int(velocities[direction, 2])
        source = padded[direction, 1 - move_east:1 - move_east + slab_cells, 1 - move_north:1 - move_north + strip_cells, :]
        source = jnp.roll(source, move_up, axis=2)
        bounce = padded[opposite[direction], 1:1 + slab_cells, 1:1 + strip_cells, :]
        anchor_row = global_rows - move_north
        anchor_cell = column_cells - move_up
        outside = ((anchor_row < 0) | (anchor_row >= total_rows))[:, None] | ((anchor_cell < 0) | (anchor_cell >= height))[None, :]
        result.append(jnp.where(outside[None], bounce, source))
    return jnp.stack(result)


def fluid_speed(fields, forcing):
    density, momentum = moments(fields)
    return (momentum + 0.5 * forcing) / density


def reference(populations, marker_weights, marker_force, owner_device, stencil_base, block_swimmer):
    weights_wide = marker_weights.astype(jnp.float32)
    patches = jnp.einsum('bcm,bkm->bkc', weights_wide, marker_force.astype(jnp.float32), precision=lax.Precision.HIGHEST)
    owner_rank = owner_device[:, 0]
    corner_slab = (owner_rank // N_GY) * CX + stencil_base[:, 0]
    corner_strip = (owner_rank % N_GY) * CY + stencil_base[:, 1]
    corner_column = stencil_base[:, 2]
    anchor_zero = jnp.zeros((), jnp.int32)

    def place_patch(force_grid, block_item):
        patch, slab_at, strip_at, column_at = block_item
        patch_cube = patch.reshape(3, STEN, STEN, STEN)
        start = (anchor_zero, slab_at.astype(jnp.int32), strip_at.astype(jnp.int32), column_at.astype(jnp.int32))
        existing = lax.dynamic_slice(force_grid, start, (3, STEN, STEN, STEN))
        return lax.dynamic_update_slice(force_grid, existing + patch_cube, start), None

    forcing, _ = lax.scan(place_patch, jnp.zeros((3, NX, NY, NZ), jnp.float32), (patches, corner_slab, corner_strip, corner_column))
    fields = populations
    for substep in range(2):
        relaxed = collide(fields, forcing)
        padded = jnp.pad(relaxed, ((0, 0), (1, 1), (1, 1), (0, 0)), mode='wrap')
        fields = stream(padded, 0, NY)
    velocity_field = fluid_speed(fields, forcing)

    def sample_cube(slab_at, strip_at, column_at):
        start = (anchor_zero, slab_at.astype(jnp.int32), strip_at.astype(jnp.int32), column_at.astype(jnp.int32))
        return lax.dynamic_slice(velocity_field, start, (3, STEN, STEN, STEN)).reshape(3, STEN * STEN * STEN)

    samples = jax.vmap(sample_cube)(corner_slab, corner_strip, corner_column)
    cell_speed = lax.optimization_barrier(samples.astype(jnp.bfloat16)).astype(jnp.float32)
    marker_velocity = speed_scale * jnp.einsum('bcm,bkc->bkm', weights_wide, cell_speed, precision=lax.Precision.HIGHEST)
    block_mean = jnp.mean(marker_velocity, axis=2)
    swimmer_velocity = jax.ops.segment_sum(block_mean, block_swimmer, SWIMMERS).T
    return fields, marker_velocity, swimmer_velocity
```

```python
import jax
import jax.numpy as jnp
from jax import lax
from jax.experimental import pallas as pl
from jax.experimental.pallas import tpu as pltpu
from jax.sharding import PartitionSpec as P

MESH = pl.DeviceIdType.MESH
F32 = jnp.float32
BF16 = jnp.bfloat16

NGX, NGY, NDEV = 16, 8, 128
CX, CY, NZ = 4, 32, 128
HELD = 48
TOP = 8

VEL = (
    (0, 0, 0),
    (1, 0, 0), (-1, 0, 0), (0, 1, 0), (0, -1, 0), (0, 0, 1), (0, 0, -1),
    (1, 1, 0), (-1, -1, 0), (1, -1, 0), (-1, 1, 0),
    (1, 0, 1), (-1, 0, -1), (1, 0, -1), (-1, 0, 1),
    (0, 1, 1), (0, -1, -1), (0, 1, -1), (0, -1, 1),
)
OPP = (0, 2, 1, 4, 3, 6, 5, 8, 7, 10, 9, 12, 11, 14, 13, 16, 15, 18, 17)
WEIGHT = (1.0 / 3.0,) + (1.0 / 18.0,) * 6 + (1.0 / 36.0,) * 12
PAIRS = ((1, 2), (3, 4), (5, 6), (7, 8), (9, 10), (11, 12), (13, 14), (15, 16), (17, 18))

XP = (1, 7, 9, 11, 13)
XM = (2, 8, 10, 12, 14)
REST = (0, 3, 4, 5, 6, 15, 16, 17, 18)
ORDER = XP + XM + REST
AT = {d: i for i, d in enumerate(ORDER)}
YP = (3, 7, 10, 15, 17)
YM = (4, 8, 9, 16, 18)


def iota(shape, dim):
    return lax.broadcasted_iota(jnp.int32, shape, dim)


def dot(a, b):
    return jnp.dot(a, b, preferred_element_type=F32)


def dot_nt(a, b):
    return lax.dot_general(a, b, (((1,), (1,)), ((), ())), preferred_element_type=F32)


def moments(f):
    rho = f[0]
    mom = [None, None, None]
    for p, m in PAIRS:
        rho = rho + (f[p] + f[m])
        diff = f[p] - f[m]
        for k in range(3):
            if VEL[p][k] == 1:
                mom[k] = diff if mom[k] is None else mom[k] + diff
            elif VEL[p][k] == -1:
                mom[k] = mom[k] - diff
    return rho, mom


def collide(f, force):
    rho, mom = moments(f)
    inv = 1.0 / rho
    u = [(mom[k] + 0.8 * force[k]) * inv for k in range(3)]
    usq = u[0] * u[0] + u[1] * u[1] + u[2] * u[2]
    whole = 1.25 * rho
    calm = 1.0 - 1.5 * usq
    out = [None] * 19
    out[0] = (WEIGHT[0] * whole) * calm - 0.25 * f[0]
    for first, last, w in ((0, 3, 1.0 / 18.0), (3, 9, 1.0 / 36.0)):
        scaled = w * whole
        base = scaled * calm
        linear = 3.0 * scaled
        for p, m in PAIRS[first:last]:
            along = None
            for k in range(3):
                if VEL[p][k] == 1:
                    along = u[k] if along is None else along + u[k]
                elif VEL[p][k] == -1:
                    along = along - u[k]
            turn = linear * along
            even = base + 1.5 * (turn * along)
            out[p] = (even + turn) - 0.25 * f[p]
            out[m] = (even - turn) - 0.25 * f[m]
    return out


def kernel(
    pop, weights, force, owner, base, swimmer,
    new_pop, speed_out, swim_out,
    sendbuf, recvbuf, backbuf, finbuf, turned, spread_hi, spread_lo, onehot_z, forcing, pad1, pad2, fluid, sampled, samples,
    ysend, yrecv, csend, crecv,
    send_sem, recv_sem, halo_send, halo_recv,
):
    gx, gy = lax.axis_index("gx"), lax.axis_index("gy")
    me = gx * NGY + gy

    barrier = pltpu.get_barrier_semaphore()

    def greet(i, _):
        t = lax.rem(me + i, NDEV)
        pl.semaphore_signal(barrier, inc=1, device_id=(t // NGY, lax.rem(t, NGY)), device_id_type=MESH)
        return 0

    lax.fori_loop(1, NDEV, greet, 0)

    col = owner[...]
    square = (HELD, HELD)
    down, across = iota(square, 0), iota(square, 1)
    row = jnp.sum(jnp.where(down == across, col, 0), axis=0, keepdims=True)
    same = col == row
    rank_col = jnp.sum(jnp.where(same & (across < down), 1, 0), axis=1, keepdims=True)
    rank_row = jnp.sum(jnp.where(same & (down < across), 1, 0), axis=0, keepdims=True)
    slot_row = rank_row * NDEV + row
    slot_col = rank_col * NDEV + col

    lane = iota((8, 128), 1)
    left = lane < 64
    ownpart = iota((8, 512), 1) // 64 == iota((8, 512), 0)
    pulls = force[...].astype(F32)
    pulls = [pulls[:, k, :] for k in range(3)]
    corner = base[...].astype(F32)
    rows01, rows2x = [], []
    for g in range(6):
        at = slice(8 * g, 8 * g + 8)
        lhs = jnp.concatenate([pulls[k][at] for k in range(3)], axis=0).astype(BF16)
        full = dot_nt(lhs, weights[512 * g : 512 * g + 512, :])
        part = []
        for k in range(3):
            x = jnp.where(ownpart, full[8 * k : 8 * k + 8], 0.0)
            y = (x[:, 0:128] + x[:, 128:256]) + (x[:, 256:384] + x[:, 384:512])
            part.append(y + pltpu.roll(y, 64, 1))
        extra = jnp.where(lane == 64, corner[at, 1:2], jnp.where(lane == 65, corner[at, 2:3], 0.0))
        rows01.append(jnp.where(left, part[0], part[1]))
        rows2x.append(jnp.where(left, part[2], extra))
    patch = jnp.concatenate([jnp.concatenate(rows01, axis=0), jnp.concatenate(rows2x, axis=0)], axis=1)
    patch_hi = patch.astype(BF16)
    patch_lo = (patch - patch_hi.astype(F32)).astype(BF16)
    put = jnp.where(iota((256, HELD), 0) == slot_row, 1.0, 0.0).astype(BF16)
    outgoing = dot(put, patch_hi) + dot(put, patch_lo)
    for j in range(2):
        for h in range(2):
            sendbuf[:, 2 * j + h, :] = outgoing[128 * j : 128 * j + 128, 128 * h : 128 * h + 128]

    pl.semaphore_wait(barrier, NDEV - 1)

    def exchange(source, target, n):
        def send(i, _):
            t = lax.rem(me + i, NDEV)
            pltpu.make_async_remote_copy(
                source.at[t], target.at[me], send_sem.at[n], recv_sem.at[n],
                device_id=(t // NGY, lax.rem(t, NGY)), device_id_type=MESH,
            ).start()
            return 0

        lax.fori_loop(1, NDEV, send, 0)
        target[me] = source[me]

    def exchanged(source, target, n):
        pltpu.make_async_remote_copy(
            source.at[pl.ds(0, NDEV - 1)], target.at[pl.ds(0, NDEV - 1)], send_sem.at[n], recv_sem.at[n],
            device_id=(lax.rem(gx + 1, NGX), gy), device_id_type=MESH,
        ).wait()

    exchange(sendbuf, recvbuf, 0)
    exchanged(sendbuf, recvbuf, 0)

    wide = iota((128, 128), 1)
    for j in range(2):
        for h in range(2):
            got = recvbuf[:, 2 * j + h, :]
            turned[j, 128 * h : 128 * h + 128, :] = got.T
            if h == 1:
                first = got[:, 65:66].astype(jnp.int32)
                for c in range(4):
                    onehot_z[256 * c + 128 * j : 256 * c + 128 * j + 128, :] = jnp.where(
                        wide == first + c, 1.0, 0.0
                    ).astype(BF16)
    sub = iota((8, 128), 0)
    bits, inside = [], []
    for j in range(2):
        y_first = jnp.broadcast_to(turned[j, 192:193, :].astype(jnp.int32), (8, 128))
        bits.append([(y_first & n) != 0 for n in (1, 2, 4)])
        offs = [sub + 8 * v - y_first for v in range(4)]
        inside.append([(off >= 0) & (off < 4) for off in offs])

    def place(ka, _):
        rows = pl.ds(pl.multiple_of(ka * 32, 32), 32)
        for c in range(4):
            for j in range(2):
                x = turned[j, pl.ds(ka * 16 + c, 8, stride=4), :]
                for n, bit in zip((1, 2, 4), bits[j]):
                    x = jnp.where(bit, pltpu.roll(x, n, 0), x)
                hi = x.astype(BF16).astype(F32)
                lo = x - hi
                start = 256 * c + 128 * j
                for piece, ref in ((hi, spread_hi), (lo, spread_lo)):
                    ref[rows, start : start + 128] = jnp.concatenate(
                        [jnp.where(inside[j][v], piece, 0.0) for v in range(4)], axis=0
                    ).astype(BF16)
        return 0

    lax.fori_loop(0, 12, place, 0)
    forcing[...] = (dot(spread_hi[...], onehot_z[...]) + dot(spread_lo[...], onehot_z[...])).reshape(3, CX, CY, NZ)

    east, west = (lax.rem(gx + 1, NGX), gy), (lax.rem(gx + NGX - 1, NGX), gy)
    up, down_ = lax.rem(gy + 1, NGY), lax.rem(gy + NGY - 1, NGY)
    north, south = (gx, up), (gx, down_)
    corners = ((7, (east[0], up)), (8, (west[0], down_)), (9, (east[0], down_)), (10, (west[0], up)))

    zlane = iota((8, NZ), 1)
    ysub = iota((8, NZ), 0)
    at_low, at_high = gy == 0, gy == NGY - 1

    def pulled(pad, d, x, yc):
        ex, ey, ez = VEL[d]
        value = pad[AT[d], x + 1 - ex, TOP + 8 * yc - ey : TOP + 8 * yc - ey + 8, :]
        wall = []
        if ez:
            value = pltpu.roll(value, 1 if ez == 1 else NZ - 1, 1)
            wall.append(zlane == (0 if ez == 1 else NZ - 1))
        if ey == 1 and yc == 0:
            wall.append((ysub == 0) & at_low)
        if ey == -1 and yc == 3:
            wall.append((ysub == 7) & at_high)
        if wall:
            mask = wall[0] if len(wall) == 1 else wall[0] | wall[1]
            value = jnp.where(mask, pad[AT[OPP[d]], x + 1, TOP + 8 * yc : TOP + 8 * yc + 8, :], value)
        return value

    def collided(pad, f, x, yc):
        at = slice(8 * yc, 8 * yc + 8)
        out = collide(f, [forcing[k, x, at, :] for k in range(3)])
        for d in range(19):
            pad[AT[d], x + 1, TOP + 8 * yc : TOP + 8 * yc + 8, :] = out[d]

    def halo(pad, n):
        def copy(source, target, i, device):
            return pltpu.make_async_remote_copy(
                source, target, halo_send.at[n, i], halo_recv.at[n, i], device_id=device, device_id_type=MESH
            )

        rows = pl.ds(TOP, CY)
        copies = [
            copy(pad.at[0:5, CX, rows, :], pad.at[0:5, 0, rows, :], 0, east),
            copy(pad.at[5:10, 1, rows, :], pad.at[5:10, CX + 1, rows, :], 1, west),
        ]
        for c in copies:
            c.start()
        for side, dirs, edge, device in ((0, YP, TOP + CY - 1, north), (1, YM, TOP, south)):
            for i, d in enumerate(dirs):
                for x in range(CX):
                    ysend[n, side, i, x : x + 1, :] = pad[AT[d], x + 1, edge : edge + 1, :]
            c = copy(ysend.at[n, side], yrecv.at[n, side], 2 + side, device)
            c.start()
            copies.append(c)
        for i, (d, device) in enumerate(corners):
            x = CX if VEL[d][0] == 1 else 1
            y = TOP + CY - 1 if VEL[d][1] == 1 else TOP
            csend[n, i] = pad[AT[d], x, y : y + 1, :]
            c = copy(csend.at[n, i], crecv.at[n, i], 4 + i, device)
            c.start()
            copies.append(c)
        for c in copies:
            c.wait()
        for side, dirs, edge in ((0, YP, TOP - 1), (1, YM, TOP + CY)):
            for i, d in enumerate(dirs):
                for x in range(CX):
                    pad[AT[d], x + 1, edge : edge + 1, :] = yrecv[n, side, i, x : x + 1, :]
        for i, (d, device) in enumerate(corners):
            x = 0 if VEL[d][0] == 1 else CX + 1
            y = TOP - 1 if VEL[d][1] == 1 else TOP + CY
            pad[AT[d], x, y : y + 1, :] = crecv[n, i]

    def step1(x, _):
        for yc in range(4):
            collided(pad1, [pop[d, x, 8 * yc : 8 * yc + 8, :] for d in range(19)], x, yc)
        return 0

    lax.fori_loop(0, CX, step1, 0)
    halo(pad1, 0)

    def step2(x, _):
        for yc in range(4):
            collided(pad2, [pulled(pad1, d, x, yc) for d in range(19)], x, yc)
        return 0

    lax.fori_loop(0, CX, step2, 0)
    halo(pad2, 1)

    def step3(x, _):
        parts = [[], [], []]
        for yc in range(4):
            f = [pulled(pad2, d, x, yc) for d in range(19)]
            at = slice(8 * yc, 8 * yc + 8)
            for d in range(19):
                new_pop[d, x, at, :] = f[d]
            rho, mom = moments(f)
            inv = 1.0 / rho
            for k in range(3):
                parts[k].append((mom[k] + 0.5 * forcing[k, x, at, :]) * inv)
        for k in range(3):
            fluid[pl.ds(pl.multiple_of(k * 128 + x * 32, 32), 32), :] = jnp.concatenate(parts[k], axis=0).astype(BF16)
        return 0

    lax.fori_loop(0, CX, step3, 0)

    sampled[...] = dot_nt(fluid[...], onehot_z[...])
    for j in range(2):
        samples[j, 192:256, :] = jnp.zeros((64, 128), F32)

    def sample(ka, _):
        for c in range(4):
            for j in range(2):
                cols = slice(256 * c + 128 * j, 256 * c + 128 * j + 128)
                x = sampled[pl.ds(pl.multiple_of(ka * 32, 32), 8), cols]
                for v in range(1, 4):
                    x = jnp.where(inside[j][v], sampled[pl.ds(pl.multiple_of(ka * 32 + 8 * v, 8), 8), cols], x)
                for n, bit in zip((1, 2, 4), bits[j]):
                    x = jnp.where(bit, pltpu.roll(x, 8 - n, 0), x)
                samples[j, pl.ds(ka * 16 + c, 4, stride=4), :] = x[0:4]
        return 0

    lax.fori_loop(0, 12, sample, 0)
    for j in range(2):
        for h in range(2):
            backbuf[:, 2 * j + h, :] = samples[j, 128 * h : 128 * h + 128, :].T
    exchange(backbuf, finbuf, 1)
    exchanged(backbuf, finbuf, 1)

    back = jnp.concatenate(
        [jnp.concatenate([finbuf[:, 2 * j + h, :] for h in range(2)], axis=1) for j in range(2)], axis=0
    ).astype(BF16)
    take = jnp.where(iota((HELD, 256), 1) == slot_col, 1.0, 0.0).astype(BF16)
    cells = dot(take, back)
    means = [[], [], []]
    for g in range(6):
        at = slice(8 * g, 8 * g + 8)
        pair, third = cells[at, 0:128], cells[at, 128:256]
        swapped = pltpu.roll(pair, 64, 1)
        each = (jnp.where(left, pair, swapped), jnp.where(left, swapped, pair), jnp.where(left, third, pltpu.roll(third, 64, 1)))
        lhs = jnp.concatenate(
            [jnp.where(ownpart, jnp.concatenate([e] * 4, axis=1), 0.0) for e in each], axis=0
        ).astype(BF16)
        result = 20.0 * dot(lhs, weights[512 * g : 512 * g + 512, :])
        for k in range(3):
            part = result[8 * k : 8 * k + 8]
            speed_out[at, k, :] = part
            means[k].append(jnp.sum(part, axis=1, keepdims=True) * (1.0 / 128.0))
    mine = jnp.sum(jnp.where(down == across, swimmer[...], 0), axis=1, keepdims=True)
    member = jnp.where(lax.rem(mine, 4) == iota((HELD, 4), 1), 1.0, 0.0)
    swim_out[...] = jnp.concatenate(
        [jnp.sum(jnp.concatenate(means[k], axis=0) * member, axis=0, keepdims=True) for k in range(3)], axis=0
    )


def body(populations, marker_weights, marker_force, owner_device, stencil_base, block_swimmer):
    vmem = pl.BlockSpec(memory_space=pltpu.VMEM)
    return pl.pallas_call(
        kernel,
        out_shape=(
            jax.ShapeDtypeStruct((19, CX, CY, NZ), F32),
            jax.ShapeDtypeStruct((HELD, 3, 128), F32),
            jax.ShapeDtypeStruct((3, 4), F32),
        ),
        in_specs=[vmem] * 6,
        out_specs=(vmem,) * 3,
        scratch_shapes=[
            pltpu.VMEM((NDEV, 4, 128), F32),
            pltpu.VMEM((NDEV, 4, 128), F32),
            pltpu.VMEM((NDEV, 4, 128), F32),
            pltpu.VMEM((NDEV, 4, 128), F32),
            pltpu.VMEM((2, 256, 128), F32),
            pltpu.VMEM((384, 1024), BF16),
            pltpu.VMEM((384, 1024), BF16),
            pltpu.VMEM((1024, 128), BF16),
            pltpu.VMEM((3, CX, CY, NZ), F32),
            pltpu.VMEM((19, CX + 2, CY + 16, NZ), F32),
            pltpu.VMEM((19, CX + 2, CY + 16, NZ), F32),
            pltpu.VMEM((384, 128), BF16),
            pltpu.VMEM((384, 1024), F32),
            pltpu.VMEM((2, 256, 128), F32),
            pltpu.VMEM((2, 2, 5, 4, 128), F32),
            pltpu.VMEM((2, 2, 5, 4, 128), F32),
            pltpu.VMEM((2, 4, 1, 128), F32),
            pltpu.VMEM((2, 4, 1, 128), F32),
            pltpu.SemaphoreType.DMA((2,)),
            pltpu.SemaphoreType.DMA((2,)),
            pltpu.SemaphoreType.DMA((2, 8)),
            pltpu.SemaphoreType.DMA((2, 8)),
        ],
        compiler_params=pltpu.CompilerParams(
            collective_id=0, has_side_effects=True, vmem_limit_bytes=40 * 1024 * 1024
        ),
    )(
        populations,
        marker_weights.reshape(HELD * 64, 128),
        marker_force,
        owner_device,
        stencil_base,
        block_swimmer.reshape(1, HELD),
    )


def solution(mesh):
    in_specs = (
        P(None, "gx", "gy", None),
        P(("gx", "gy"), None, None),
        P(("gx", "gy"), None, None),
        P(("gx", "gy"), None),
        P(("gx", "gy"), None),
        P(("gx", "gy")),
    )
    out_specs = (P(None, "gx", "gy", None), P(("gx", "gy"), None, None), P(None, ("gx", "gy")))
    return jax.shard_map(body, mesh=mesh, in_specs=in_specs, out_specs=out_specs, check_vma=False)
```

```python
import jax
import jax.numpy as jnp
from jax import lax
from jax.experimental import pallas as pl
from jax.experimental.pallas import tpu as pltpu
from jax.sharding import PartitionSpec as P

MESH = pl.DeviceIdType.MESH
F32 = jnp.float32
BF16 = jnp.bfloat16

NGX, NGY, NDEV = 16, 8, 128
CX, CY, NZ = 4, 32, 128
HELD = 48
TOP = 8

VEL = (
    (0, 0, 0),
    (1, 0, 0), (-1, 0, 0), (0, 1, 0), (0, -1, 0), (0, 0, 1), (0, 0, -1),
    (1, 1, 0), (-1, -1, 0), (1, -1, 0), (-1, 1, 0),
    (1, 0, 1), (-1, 0, -1), (1, 0, -1), (-1, 0, 1),
    (0, 1, 1), (0, -1, -1), (0, 1, -1), (0, -1, 1),
)
OPP = (0, 2, 1, 4, 3, 6, 5, 8, 7, 10, 9, 12, 11, 14, 13, 16, 15, 18, 17)
WEIGHT = (1.0 / 3.0,) + (1.0 / 18.0,) * 6 + (1.0 / 36.0,) * 12
PAIRS = ((1, 2), (3, 4), (5, 6), (7, 8), (9, 10), (11, 12), (13, 14), (15, 16), (17, 18))

XP = (1, 7, 9, 11, 13)
XM = (2, 8, 10, 12, 14)
REST = (0, 3, 4, 5, 6, 15, 16, 17, 18)
ORDER = XP + XM + REST
AT = {d: i for i, d in enumerate(ORDER)}
YP = (3, 7, 10, 15, 17)
YM = (4, 8, 9, 16, 18)


def iota(shape, dim):
    return lax.broadcasted_iota(jnp.int32, shape, dim)


def dot(a, b):
    return jnp.dot(a, b, preferred_element_type=F32)


def dot_nt(a, b):
    return lax.dot_general(a, b, (((1,), (1,)), ((), ())), preferred_element_type=F32)


def moments(f):
    rho = f[0]
    mom = [None, None, None]
    for p, m in PAIRS:
        rho = rho + (f[p] + f[m])
        diff = f[p] - f[m]
        for k in range(3):
            if VEL[p][k] == 1:
                mom[k] = diff if mom[k] is None else mom[k] + diff
            elif VEL[p][k] == -1:
                mom[k] = mom[k] - diff
    return rho, mom


def collide(f, force):
    rho, mom = moments(f)
    inv = 1.0 / rho
    u = [(mom[k] + 0.8 * force[k]) * inv for k in range(3)]
    usq = u[0] * u[0] + u[1] * u[1] + u[2] * u[2]
    whole = 1.25 * rho
    calm = 1.0 - 1.5 * usq
    out = [None] * 19
    out[0] = (WEIGHT[0] * whole) * calm - 0.25 * f[0]
    for first, last, w in ((0, 3, 1.0 / 18.0), (3, 9, 1.0 / 36.0)):
        scaled = w * whole
        base = scaled * calm
        linear = 3.0 * scaled
        for p, m in PAIRS[first:last]:
            along = None
            for k in range(3):
                if VEL[p][k] == 1:
                    along = u[k] if along is None else along + u[k]
                elif VEL[p][k] == -1:
                    along = along - u[k]
            turn = linear * along
            even = base + 1.5 * (turn * along)
            out[p] = (even + turn) - 0.25 * f[p]
            out[m] = (even - turn) - 0.25 * f[m]
    return out


def kernel(
    pop_hbm, weights_hbm, force_hbm, owner_hbm, base_hbm, swimmer_hbm,
    new_pop, speed_out, swim_out,
    pop, weights, force, owner, base, swimmer,
    sendbuf, recvbuf, backbuf, finbuf, turned, spread_hi, spread_lo, onehot_z, forcing, pad1, pad2, fluid, sampled, samples,
    ysend, yrecv, csend, crecv,
    load_sem, send_sem, recv_sem, halo_send, halo_recv,
):
    loads = [
        pltpu.make_async_copy(source, target, load_sem.at[i])
        for i, (source, target) in enumerate(
            ((owner_hbm, owner), (base_hbm, base), (force_hbm, force), (weights_hbm, weights), (swimmer_hbm, swimmer), (pop_hbm, pop))
        )
    ]
    for load in loads:
        load.start()

    gx, gy = lax.axis_index("gx"), lax.axis_index("gy")
    me = gx * NGY + gy
    core, my_x = lax.rem(gx, 2), lax.rem(lax.div(gx, 2), 4)
    my_y, my_z = lax.div(gy, 2), lax.div(gx, 8) * 2 + lax.rem(gy, 2)

    def chip(dx, dy, dz):
        z = lax.rem(my_z + dz, 4)
        return lax.div(z, 2) * 8 + lax.rem(my_x + dx, 4) * 2, lax.rem(my_y + dy, 4) * 2 + lax.rem(z, 2)

    def to_all(act):
        def offset(digit):
            return jnp.where(digit < 2, 2 * digit + 1, 6 - 2 * digit)

        def step(i, _):
            tx, ty = chip(offset(lax.rem(i, 4)), offset(lax.rem(lax.div(i, 4), 4)), offset(lax.div(i, 16)))
            act(tx, ty)
            act(tx + 1, ty)
            return 0

        lax.fori_loop(0, 63, step, 0)
        act(gx + 1 - 2 * core, gy)

    barrier = pltpu.get_barrier_semaphore()
    to_all(lambda tx, ty: pl.semaphore_signal(barrier, inc=1, device_id=(tx, ty), device_id_type=MESH))

    for load in loads[:4]:
        load.wait()
    square = (HELD, HELD)
    down, across = iota(square, 0), iota(square, 1)

    def standing(line):
        return jnp.sum(jnp.where(down == across, line, 0), axis=1, keepdims=True)

    row = owner[...]
    col = standing(row)
    same = col == row
    rank_col = jnp.sum(jnp.where(same & (across < down), 1, 0), axis=1, keepdims=True)
    rank_row = jnp.sum(jnp.where(same & (down < across), 1, 0), axis=0, keepdims=True)
    slot_row = rank_row * NDEV + row
    slot_col = rank_col * NDEV + col

    lane = iota((8, 128), 1)
    left = lane < 64
    ownpart = iota((8, 512), 1) // 64 == iota((8, 512), 0)
    pulls = [force[k].astype(F32) for k in range(3)]
    strip = standing(base[1:2, :]).astype(F32)
    column = standing(base[2:3, :]).astype(F32)
    rows01, rows2x = [], []
    for g in range(6):
        at = slice(8 * g, 8 * g + 8)
        lhs = jnp.concatenate([pulls[k][at] for k in range(3)], axis=0).astype(BF16)
        full = dot_nt(lhs, weights[512 * g : 512 * g + 512, :])
        part = []
        for k in range(3):
            x = jnp.where(ownpart, full[8 * k : 8 * k + 8], 0.0)
            y = (x[:, 0:128] + x[:, 128:256]) + (x[:, 256:384] + x[:, 384:512])
            part.append(y + pltpu.roll(y, 64, 1))
        extra = jnp.where(lane == 64, strip[at], jnp.where(lane == 65, column[at], 0.0))
        rows01.append(jnp.where(left, part[0], part[1]))
        rows2x.append(jnp.where(left, part[2], extra))
    patch = jnp.concatenate([jnp.concatenate(rows01, axis=0), jnp.concatenate(rows2x, axis=0)], axis=1)
    patch_hi = patch.astype(BF16)
    patch_lo = (patch - patch_hi.astype(F32)).astype(BF16)
    put = jnp.where(iota((256, HELD), 0) == slot_row, 1.0, 0.0).astype(BF16)
    outgoing = dot(put, patch_hi) + dot(put, patch_lo)
    for j in range(2):
        for h in range(2):
            sendbuf[:, 2 * j + h, :] = outgoing[128 * j : 128 * j + 128, 128 * h : 128 * h + 128]

    pl.semaphore_wait(barrier, NDEV - 1)

    def exchange(source, target, n):
        to_all(
            lambda tx, ty: pltpu.make_async_remote_copy(
                source.at[tx * NGY + ty], target.at[me], send_sem.at[n], recv_sem.at[n],
                device_id=(tx, ty), device_id_type=MESH,
            ).start()
        )
        target[me] = source[me]

    def exchanged(source, target, n):
        return pltpu.make_async_remote_copy(
            source.at[pl.ds(0, NDEV - 1)], target.at[pl.ds(0, NDEV - 1)], send_sem.at[n], recv_sem.at[n],
            device_id=(lax.rem(gx + 1, NGX), gy), device_id_type=MESH,
        )

    exchange(sendbuf, recvbuf, 0)
    exchanged(sendbuf, recvbuf, 0).wait_recv()

    wide = iota((128, 128), 1)
    for j in range(2):
        for h in range(2):
            got = recvbuf[:, 2 * j + h, :]
            turned[j, 128 * h : 128 * h + 128, :] = got.T
            if h == 1:
                first = got[:, 65:66].astype(jnp.int32)
                for c in range(4):
                    onehot_z[256 * c + 128 * j : 256 * c + 128 * j + 128, :] = jnp.where(
                        wide == first + c, 1.0, 0.0
                    ).astype(BF16)
    sub = iota((8, 128), 0)
    bits, inside = [], []
    for j in range(2):
        y_first = jnp.broadcast_to(turned[j, 192:193, :].astype(jnp.int32), (8, 128))
        bits.append([(y_first & n) != 0 for n in (1, 2, 4)])
        offs = [sub + 8 * v - y_first for v in range(4)]
        inside.append([(off >= 0) & (off < 4) for off in offs])

    def place(ka, _):
        rows = pl.ds(pl.multiple_of(ka * 32, 32), 32)
        for c in range(4):
            for j in range(2):
                x = turned[j, pl.ds(ka * 16 + c, 8, stride=4), :]
                for n, bit in zip((1, 2, 4), bits[j]):
                    x = jnp.where(bit, pltpu.roll(x, n, 0), x)
                hi = x.astype(BF16).astype(F32)
                lo = x - hi
                start = 256 * c + 128 * j
                for piece, ref in ((hi, spread_hi), (lo, spread_lo)):
                    ref[rows, start : start + 128] = jnp.concatenate(
                        [jnp.where(inside[j][v], piece, 0.0) for v in range(4)], axis=0
                    ).astype(BF16)
        return 0

    lax.fori_loop(0, 12, place, 0)
    forcing[...] = (dot(spread_hi[...], onehot_z[...]) + dot(spread_lo[...], onehot_z[...])).reshape(3, CX, CY, NZ)

    east, west = (lax.rem(gx + 1, NGX), gy), (lax.rem(gx + NGX - 1, NGX), gy)
    up, down_ = lax.rem(gy + 1, NGY), lax.rem(gy + NGY - 1, NGY)
    north, south = (gx, up), (gx, down_)
    corners = ((7, (east[0], up)), (8, (west[0], down_)), (9, (east[0], down_)), (10, (west[0], up)))

    zlane = iota((8, NZ), 1)
    ysub = iota((8, NZ), 0)
    at_low, at_high = gy == 0, gy == NGY - 1

    def pulled(pad, d, x, yc):
        ex, ey, ez = VEL[d]
        value = pad[AT[d], x + 1 - ex, TOP + 8 * yc - ey : TOP + 8 * yc - ey + 8, :]
        wall = []
        if ez:
            value = pltpu.roll(value, 1 if ez == 1 else NZ - 1, 1)
            wall.append(zlane == (0 if ez == 1 else NZ - 1))
        if ey == 1 and yc == 0:
            wall.append((ysub == 0) & at_low)
        if ey == -1 and yc == 3:
            wall.append((ysub == 7) & at_high)
        if wall:
            mask = wall[0] if len(wall) == 1 else wall[0] | wall[1]
            value = jnp.where(mask, pad[AT[OPP[d]], x + 1, TOP + 8 * yc : TOP + 8 * yc + 8, :], value)
        return value

    def collided(pad, f, x, yc):
        at = slice(8 * yc, 8 * yc + 8)
        out = collide(f, [forcing[k, x, at, :] for k in range(3)])
        for d in range(19):
            pad[AT[d], x + 1, TOP + 8 * yc : TOP + 8 * yc + 8, :] = out[d]

    def halo_start(pad, n):
        def copy(source, target, i, device):
            c = pltpu.make_async_remote_copy(
                source, target, halo_send.at[n, i], halo_recv.at[n, i], device_id=device, device_id_type=MESH
            )
            c.start()
            return c

        rows = pl.ds(TOP, CY)
        copies = []
        for i, (d, device) in enumerate(corners):
            x = CX if VEL[d][0] == 1 else 1
            y = TOP + CY - 1 if VEL[d][1] == 1 else TOP
            csend[n, i] = pad[AT[d], x, y : y + 1, :]
            copies.append(copy(csend.at[n, i], crecv.at[n, i], 4 + i, device))
        copies.append(copy(pad.at[0:5, CX, rows, :], pad.at[0:5, 0, rows, :], 0, east))
        copies.append(copy(pad.at[5:10, 1, rows, :], pad.at[5:10, CX + 1, rows, :], 1, west))
        for side, dirs, edge, device in ((0, YP, TOP + CY - 1, north), (1, YM, TOP, south)):
            for i, d in enumerate(dirs):
                for x in range(CX):
                    ysend[n, side, i, x : x + 1, :] = pad[AT[d], x + 1, edge : edge + 1, :]
            copies.append(copy(ysend.at[n, side], yrecv.at[n, side], 2 + side, device))
        return copies

    def halo_finish(pad, n, copies):
        for c in copies:
            c.wait_recv()
        for side, dirs, edge in ((0, YP, TOP - 1), (1, YM, TOP + CY)):
            for i, d in enumerate(dirs):
                for x in range(CX):
                    pad[AT[d], x + 1, edge : edge + 1, :] = yrecv[n, side, i, x : x + 1, :]
        for i, (d, device) in enumerate(corners):
            x = 0 if VEL[d][0] == 1 else CX + 1
            y = TOP - 1 if VEL[d][1] == 1 else TOP + CY
            pad[AT[d], x, y : y + 1, :] = crecv[n, i]

    def rim(work):
        def sides(i, _):
            for yc in range(4):
                work(i * (CX - 1), yc)
            return 0

        def middle(x, _):
            work(x, 0)
            work(x, 3)
            return 0

        lax.fori_loop(0, 2, sides, 0)
        lax.fori_loop(1, CX - 1, middle, 0)

    def core_cells(work):
        def middle(x, _):
            work(x, 1)
            work(x, 2)
            return 0

        lax.fori_loop(1, CX - 1, middle, 0)

    def step1(x, yc):
        collided(pad1, [pop[d, x, 8 * yc : 8 * yc + 8, :] for d in range(19)], x, yc)

    def step2(x, yc):
        collided(pad2, [pulled(pad1, d, x, yc) for d in range(19)], x, yc)

    def step3(x, yc):
        f = [pulled(pad2, d, x, yc) for d in range(19)]
        at = slice(8 * yc, 8 * yc + 8)
        for d in range(19):
            new_pop[d, x, at, :] = f[d]
        rho, mom = moments(f)
        inv = 1.0 / rho
        for k in range(3):
            fluid[k, x, at, :] = (mom[k] + 0.5 * forcing[k, x, at, :]) * inv

    loads[5].wait()
    rim(step1)
    halo1 = halo_start(pad1, 0)
    core_cells(step1)
    core_cells(step2)
    halo_finish(pad1, 0, halo1)
    rim(step2)
    halo2 = halo_start(pad2, 1)
    core_cells(step3)
    halo_finish(pad2, 1, halo2)
    rim(step3)

    sampled[...] = dot_nt(fluid[...].reshape(384, NZ).astype(BF16), onehot_z[...])
    for j in range(2):
        samples[j, 192:256, :] = jnp.zeros((64, 128), F32)

    def sample(ka, _):
        for c in range(4):
            for j in range(2):
                cols = slice(256 * c + 128 * j, 256 * c + 128 * j + 128)
                x = sampled[pl.ds(pl.multiple_of(ka * 32, 32), 8), cols]
                for v in range(1, 4):
                    x = jnp.where(inside[j][v], sampled[pl.ds(pl.multiple_of(ka * 32 + 8 * v, 8), 8), cols], x)
                for n, bit in zip((1, 2, 4), bits[j]):
                    x = jnp.where(bit, pltpu.roll(x, 8 - n, 0), x)
                samples[j, pl.ds(ka * 16 + c, 4, stride=4), :] = x[0:4]
        return 0

    lax.fori_loop(0, 12, sample, 0)
    for j in range(2):
        for h in range(2):
            backbuf[:, 2 * j + h, :] = samples[j, 128 * h : 128 * h + 128, :].T
    exchange(backbuf, finbuf, 1)
    exchanged(backbuf, finbuf, 1).wait_recv()

    back = jnp.concatenate(
        [jnp.concatenate([finbuf[:, 2 * j + h, :] for h in range(2)], axis=1) for j in range(2)], axis=0
    ).astype(BF16)
    take = jnp.where(iota((HELD, 256), 1) == slot_col, 1.0, 0.0).astype(BF16)
    cells = dot(take, back)
    means = [[], [], []]
    for g in range(6):
        at = slice(8 * g, 8 * g + 8)
        pair, third = cells[at, 0:128], cells[at, 128:256]
        swapped = pltpu.roll(pair, 64, 1)
        each = (jnp.where(left, pair, swapped), jnp.where(left, swapped, pair), jnp.where(left, third, pltpu.roll(third, 64, 1)))
        lhs = jnp.concatenate(
            [jnp.where(ownpart, jnp.concatenate([e] * 4, axis=1), 0.0) for e in each], axis=0
        ).astype(BF16)
        result = 20.0 * dot(lhs, weights[512 * g : 512 * g + 512, :])
        for k in range(3):
            part = result[8 * k : 8 * k + 8]
            speed_out[k, at, :] = part
            means[k].append(jnp.sum(part, axis=1, keepdims=True) * (1.0 / 128.0))
    loads[4].wait()
    mine = standing(swimmer[...])
    member = jnp.where(lax.rem(mine, 4) == iota((HELD, 4), 1), 1.0, 0.0)
    swim_out[...] = jnp.concatenate(
        [jnp.sum(jnp.concatenate(means[k], axis=0) * member, axis=0, keepdims=True) for k in range(3)], axis=0
    )

    exchanged(sendbuf, recvbuf, 0).wait_send()
    exchanged(backbuf, finbuf, 1).wait_send()
    for c in halo1 + halo2:
        c.wait_send()


def body(populations, marker_weights, marker_force, owner_device, stencil_base, block_swimmer):
    vmem = pl.BlockSpec(memory_space=pltpu.VMEM)
    hbm = pl.BlockSpec(memory_space=pl.ANY)
    operands = (
        populations,
        marker_weights.reshape(HELD * 64, 128),
        marker_force.transpose(1, 0, 2),
        owner_device.reshape(1, HELD),
        stencil_base.T,
        block_swimmer.reshape(1, HELD),
    )
    fields, speed, swim = pl.pallas_call(
        kernel,
        out_shape=(
            jax.ShapeDtypeStruct((19, CX, CY, NZ), F32),
            jax.ShapeDtypeStruct((3, HELD, 128), F32),
            jax.ShapeDtypeStruct((3, 4), F32),
        ),
        in_specs=[hbm] * 6,
        out_specs=(vmem,) * 3,
        scratch_shapes=[
            pltpu.VMEM((19, CX, CY, NZ), F32),
            pltpu.VMEM((HELD * 64, 128), BF16),
            pltpu.VMEM((3, HELD, 128), BF16),
            pltpu.VMEM((1, HELD), jnp.int32),
            pltpu.VMEM((3, HELD), jnp.int32),
            pltpu.VMEM((1, HELD), jnp.int32),
            pltpu.VMEM((NDEV, 4, 128), F32),
            pltpu.VMEM((NDEV, 4, 128), F32),
            pltpu.VMEM((NDEV, 4, 128), F32),
            pltpu.VMEM((NDEV, 4, 128), F32),
            pltpu.VMEM((2, 256, 128), F32),
            pltpu.VMEM((384, 1024), BF16),
            pltpu.VMEM((384, 1024), BF16),
            pltpu.VMEM((1024, 128), BF16),
            pltpu.VMEM((3, CX, CY, NZ), F32),
            pltpu.VMEM((19, CX + 2, CY + 16, NZ), F32),
            pltpu.VMEM((19, CX + 2, CY + 16, NZ), F32),
            pltpu.VMEM((3, CX, CY, NZ), F32),
            pltpu.VMEM((384, 1024), F32),
            pltpu.VMEM((2, 256, 128), F32),
            pltpu.VMEM((2, 2, 5, 4, 128), F32),
            pltpu.VMEM((2, 2, 5, 4, 128), F32),
            pltpu.VMEM((2, 4, 1, 128), F32),
            pltpu.VMEM((2, 4, 1, 128), F32),
            pltpu.SemaphoreType.DMA((6,)),
            pltpu.SemaphoreType.DMA((2,)),
            pltpu.SemaphoreType.DMA((2,)),
            pltpu.SemaphoreType.DMA((2, 8)),
            pltpu.SemaphoreType.DMA((2, 8)),
        ],
        compiler_params=pltpu.CompilerParams(
            collective_id=0, has_side_effects=True, vmem_limit_bytes=40 * 1024 * 1024
        ),
    )(
        *(pltpu.with_memory_space_constraint(x, pltpu.HBM) for x in operands)
    )
    return fields, speed.transpose(1, 0, 2), swim


def solution(mesh):
    in_specs = (
        P(None, "gx", "gy", None),
        P(("gx", "gy"), None, None),
        P(("gx", "gy"), None, None),
        P(("gx", "gy"), None),
        P(("gx", "gy"), None),
        P(("gx", "gy")),
    )
    out_specs = (P(None, "gx", "gy", None), P(("gx", "gy"), None, None), P(None, ("gx", "gy")))
    return jax.shard_map(body, mesh=mesh, in_specs=in_specs, out_specs=out_specs, check_vma=False)
```

```python
import jax
import jax.numpy as jnp
from jax import lax
from jax.experimental import pallas as pl
from jax.experimental.pallas import tpu as pltpu
from jax.sharding import PartitionSpec as P

MESH = pl.DeviceIdType.MESH
F32 = jnp.float32
BF16 = jnp.bfloat16

NGX, NGY, NDEV = 16, 8, 128
CX, CY, NZ = 4, 32, 128
HELD = 48
TOP = 8

VEL = (
    (0, 0, 0),
    (1, 0, 0), (-1, 0, 0), (0, 1, 0), (0, -1, 0), (0, 0, 1), (0, 0, -1),
    (1, 1, 0), (-1, -1, 0), (1, -1, 0), (-1, 1, 0),
    (1, 0, 1), (-1, 0, -1), (1, 0, -1), (-1, 0, 1),
    (0, 1, 1), (0, -1, -1), (0, 1, -1), (0, -1, 1),
)
OPP = (0, 2, 1, 4, 3, 6, 5, 8, 7, 10, 9, 12, 11, 14, 13, 16, 15, 18, 17)
WEIGHT = (1.0 / 3.0,) + (1.0 / 18.0,) * 6 + (1.0 / 36.0,) * 12
PAIRS = ((1, 2), (3, 4), (5, 6), (7, 8), (9, 10), (11, 12), (13, 14), (15, 16), (17, 18))

XP = (1, 7, 9, 11, 13)
XM = (2, 8, 10, 12, 14)
REST = (0, 3, 4, 5, 6, 15, 16, 17, 18)
ORDER = XP + XM + REST
AT = {d: i for i, d in enumerate(ORDER)}
YP = (3, 7, 10, 15, 17)
YM = (4, 8, 9, 16, 18)


def iota(shape, dim):
    return lax.broadcasted_iota(jnp.int32, shape, dim)


def dot(a, b):
    return jnp.dot(a, b, preferred_element_type=F32)


def dot_nt(a, b):
    return lax.dot_general(a, b, (((1,), (1,)), ((), ())), preferred_element_type=F32)


def own_part():
    return lax.div(iota((8, 512), 1), 64) == iota((8, 512), 0)


def moments(f):
    rho = f[0]
    mom = [None, None, None]
    for p, m in PAIRS:
        rho = rho + (f[p] + f[m])
        diff = f[p] - f[m]
        for k in range(3):
            if VEL[p][k] == 1:
                mom[k] = diff if mom[k] is None else mom[k] + diff
            elif VEL[p][k] == -1:
                mom[k] = mom[k] - diff
    return rho, mom


def collide(f, force):
    rho, mom = moments(f)
    inv = 1.0 / rho
    u = [(mom[k] + 0.8 * force[k]) * inv for k in range(3)]
    usq = u[0] * u[0] + u[1] * u[1] + u[2] * u[2]
    whole = 1.25 * rho
    calm = 1.0 - 1.5 * usq
    out = [None] * 19
    out[0] = (WEIGHT[0] * whole) * calm - 0.25 * f[0]
    for first, last, w in ((0, 3, 1.0 / 18.0), (3, 9, 1.0 / 36.0)):
        scaled = w * whole
        base = scaled * calm
        linear = 3.0 * scaled
        for p, m in PAIRS[first:last]:
            along = None
            for k in range(3):
                if VEL[p][k] == 1:
                    along = u[k] if along is None else along + u[k]
                elif VEL[p][k] == -1:
                    along = along - u[k]
            turn = linear * along
            even = base + 1.5 * (turn * along)
            out[p] = (even + turn) - 0.25 * f[p]
            out[m] = (even - turn) - 0.25 * f[m]
    return out


def kernel(
    pop_hbm, weights_hbm, force_hbm, owner_hbm, base_hbm, swimmer_hbm,
    new_pop, finbuf, weights, take_out, member_out,
    pop, force, owner, base, swimmer,
    sendbuf, recvbuf, backbuf, turned, spread_hi, spread_lo, onehot_z, forcing, pad1, pad2, fluid, sampled, samples,
    ysend, yrecv, csend, crecv,
    load_sem, send_sem, recv_sem, halo_send, halo_recv,
):
    loads = [
        pltpu.make_async_copy(source, target, load_sem.at[i])
        for i, (source, target) in enumerate(
            ((owner_hbm, owner), (base_hbm, base), (force_hbm, force), (weights_hbm, weights), (swimmer_hbm, swimmer), (pop_hbm, pop))
        )
    ]
    gx, gy = lax.axis_index("gx"), lax.axis_index("gy")
    me = gx * NGY + gy
    core, my_x = lax.rem(gx, 2), lax.rem(lax.div(gx, 2), 4)
    my_y, my_z = lax.div(gy, 2), lax.div(gx, 8) * 2 + lax.rem(gy, 2)

    along_x = [lax.rem(my_x + d, 4) * 2 for d in (1, 3, 2, 0)]

    def to_all(act):
        def offset(digit):
            return jnp.where(digit < 2, 2 * digit + 1, 6 - 2 * digit)

        def step(i, _):
            z = lax.rem(my_z + offset(lax.div(i, 4)), 4)
            tx = lax.div(z, 2) * 8
            ty = lax.rem(my_y + offset(lax.rem(i, 4)), 4) * 2 + lax.rem(z, 2)
            for x in along_x:
                act(tx + x, ty)
                act(tx + x + 1, ty)
            return 0

        lax.fori_loop(0, 15, step, 0)
        first = lax.div(gx, 8) * 8
        for x in along_x[:3]:
            act(first + x, gy)
            act(first + x + 1, gy)
        act(gx + 1 - 2 * core, gy)

    barrier = pltpu.get_barrier_semaphore()
    to_all(lambda tx, ty: pl.semaphore_signal(barrier, inc=1, device_id=(tx, ty), device_id_type=MESH))

    for load in loads:
        load.start()

    for load in loads[:4]:
        load.wait()
    square = (HELD, HELD)
    down, across = iota(square, 0), iota(square, 1)

    def standing(line):
        return jnp.sum(jnp.where(down == across, line, 0), axis=1, keepdims=True)

    row = owner[...]
    col = standing(row)
    same = col == row
    rank_col = jnp.sum(jnp.where(same & (across < down), 1, 0), axis=1, keepdims=True)
    rank_row = jnp.sum(jnp.where(same & (down < across), 1, 0), axis=0, keepdims=True)
    slot_row = rank_row * NDEV + row
    slot_col = rank_col * NDEV + col

    take_out[...] = jnp.where(iota((HELD, 256), 1) == slot_col, 1.0, 0.0).astype(BF16)
    loads[4].wait()
    member_out[...] = jnp.where(lax.rem(standing(swimmer[...]), 4) == iota((HELD, 4), 1), 1.0, 0.0)

    lane = iota((8, 128), 1)
    left = lane < 64
    ownpart = own_part()
    pulls = [force[k].astype(F32) for k in range(3)]
    strip = standing(base[1:2, :]).astype(F32)
    column = standing(base[2:3, :]).astype(F32)
    rows01, rows2x = [], []
    for g in range(6):
        at = slice(8 * g, 8 * g + 8)
        lhs = jnp.concatenate([pulls[k][at] for k in range(3)], axis=0).astype(BF16)
        full = dot_nt(lhs, weights[512 * g : 512 * g + 512, :])
        part = []
        for k in range(3):
            x = jnp.where(ownpart, full[8 * k : 8 * k + 8], 0.0)
            y = (x[:, 0:128] + x[:, 128:256]) + (x[:, 256:384] + x[:, 384:512])
            part.append(y + pltpu.roll(y, 64, 1))
        extra = jnp.where(lane == 64, strip[at], jnp.where(lane == 65, column[at], 0.0))
        rows01.append(jnp.where(left, part[0], part[1]))
        rows2x.append(jnp.where(left, part[2], extra))
    patch = jnp.concatenate([jnp.concatenate(rows01, axis=0), jnp.concatenate(rows2x, axis=0)], axis=1)
    patch_hi = patch.astype(BF16)
    patch_lo = (patch - patch_hi.astype(F32)).astype(BF16)
    put = jnp.where(iota((256, HELD), 0) == slot_row, 1.0, 0.0).astype(BF16)
    outgoing = dot(put, patch_hi) + dot(put, patch_lo)
    for j in range(2):
        for h in range(2):
            sendbuf[:, 2 * j + h, :] = outgoing[128 * j : 128 * j + 128, 128 * h : 128 * h + 128]

    pl.semaphore_wait(barrier, NDEV - 1)

    def exchange(source, target, n):
        to_all(
            lambda tx, ty: pltpu.make_async_remote_copy(
                source.at[tx * NGY + ty], target.at[me], send_sem.at[n], recv_sem.at[n],
                device_id=(tx, ty), device_id_type=MESH,
            ).start()
        )
        target[me] = source[me]

    def exchanged(source, target, n):
        return pltpu.make_async_remote_copy(
            source.at[pl.ds(0, NDEV - 1)], target.at[pl.ds(0, NDEV - 1)], send_sem.at[n], recv_sem.at[n],
            device_id=(lax.rem(gx + 1, NGX), gy), device_id_type=MESH,
        )

    exchange(sendbuf, recvbuf, 0)
    exchanged(sendbuf, recvbuf, 0).wait_recv()

    wide = iota((128, 128), 1)
    for j in range(2):
        for h in range(2):
            got = recvbuf[:, 2 * j + h, :]
            turned[j, 128 * h : 128 * h + 128, :] = got.T
            if h == 1:
                first = got[:, 65:66].astype(jnp.int32)
                for c in range(4):
                    onehot_z[256 * c + 128 * j : 256 * c + 128 * j + 128, :] = jnp.where(
                        wide == first + c, 1.0, 0.0
                    ).astype(BF16)
    sub = iota((8, 128), 0)
    bits, inside = [], []
    for j in range(2):
        y_first = jnp.broadcast_to(turned[j, 192:193, :].astype(jnp.int32), (8, 128))
        bits.append([(y_first & n) != 0 for n in (1, 2, 4)])
        offs = [sub + 8 * v - y_first for v in range(4)]
        inside.append([(off >= 0) & (off < 4) for off in offs])

    def place(ka, _):
        rows = pl.ds(pl.multiple_of(ka * 32, 32), 32)
        for c in range(4):
            for j in range(2):
                x = turned[j, pl.ds(ka * 16 + c, 8, stride=4), :]
                for n, bit in zip((1, 2, 4), bits[j]):
                    x = jnp.where(bit, pltpu.roll(x, n, 0), x)
                hi = x.astype(BF16).astype(F32)
                lo = x - hi
                start = 256 * c + 128 * j
                for piece, ref in ((hi, spread_hi), (lo, spread_lo)):
                    ref[rows, start : start + 128] = jnp.concatenate(
                        [jnp.where(inside[j][v], piece, 0.0) for v in range(4)], axis=0
                    ).astype(BF16)
        return 0

    lax.fori_loop(0, 12, place, 0)
    forcing[...] = (dot(spread_hi[...], onehot_z[...]) + dot(spread_lo[...], onehot_z[...])).reshape(3, CX, CY, NZ)

    east, west = (lax.rem(gx + 1, NGX), gy), (lax.rem(gx + NGX - 1, NGX), gy)
    up, down_ = lax.rem(gy + 1, NGY), lax.rem(gy + NGY - 1, NGY)
    north, south = (gx, up), (gx, down_)
    corners = ((7, (east[0], up)), (8, (west[0], down_)), (9, (east[0], down_)), (10, (west[0], up)))

    zlane = iota((8, NZ), 1)
    ysub = iota((8, NZ), 0)
    at_low, at_high = gy == 0, gy == NGY - 1

    def pulled(pad, d, x, yc):
        ex, ey, ez = VEL[d]
        value = pad[AT[d], x + 1 - ex, TOP + 8 * yc - ey : TOP + 8 * yc - ey + 8, :]
        wall = []
        if ez:
            value = pltpu.roll(value, 1 if ez == 1 else NZ - 1, 1)
            wall.append(zlane == (0 if ez == 1 else NZ - 1))
        if ey == 1 and yc == 0:
            wall.append((ysub == 0) & at_low)
        if ey == -1 and yc == 3:
            wall.append((ysub == 7) & at_high)
        if wall:
            mask = wall[0] if len(wall) == 1 else wall[0] | wall[1]
            value = jnp.where(mask, pad[AT[OPP[d]], x + 1, TOP + 8 * yc : TOP + 8 * yc + 8, :], value)
        return value

    def collided(pad, f, x, yc):
        at = slice(8 * yc, 8 * yc + 8)
        out = collide(f, [forcing[k, x, at, :] for k in range(3)])
        for d in range(19):
            pad[AT[d], x + 1, TOP + 8 * yc : TOP + 8 * yc + 8, :] = out[d]

    def halo_start(pad, n):
        def copy(source, target, i, device):
            c = pltpu.make_async_remote_copy(
                source, target, halo_send.at[n, i], halo_recv.at[n, i], device_id=device, device_id_type=MESH
            )
            c.start()
            return c

        rows = pl.ds(TOP, CY)
        copies = []
        for i, (d, device) in enumerate(corners):
            x = CX if VEL[d][0] == 1 else 1
            y = TOP + CY - 1 if VEL[d][1] == 1 else TOP
            csend[n, i] = pad[AT[d], x, y : y + 1, :]
            copies.append(copy(csend.at[n, i], crecv.at[n, i], 4 + i, device))
        copies.append(copy(pad.at[0:5, CX, rows, :], pad.at[0:5, 0, rows, :], 0, east))
        copies.append(copy(pad.at[5:10, 1, rows, :], pad.at[5:10, CX + 1, rows, :], 1, west))
        for side, dirs, edge, device in ((0, YP, TOP + CY - 1, north), (1, YM, TOP, south)):
            for i, d in enumerate(dirs):
                for x in range(CX):
                    ysend[n, side, i, x : x + 1, :] = pad[AT[d], x + 1, edge : edge + 1, :]
            copies.append(copy(ysend.at[n, side], yrecv.at[n, side], 2 + side, device))
        return copies

    def halo_finish(pad, n, copies):
        for c in copies:
            c.wait_recv()
        for side, dirs, edge in ((0, YP, TOP - 1), (1, YM, TOP + CY)):
            for i, d in enumerate(dirs):
                for x in range(CX):
                    pad[AT[d], x + 1, edge : edge + 1, :] = yrecv[n, side, i, x : x + 1, :]
        for i, (d, device) in enumerate(corners):
            x = 0 if VEL[d][0] == 1 else CX + 1
            y = TOP - 1 if VEL[d][1] == 1 else TOP + CY
            pad[AT[d], x, y : y + 1, :] = crecv[n, i]

    def rim(work):
        def sides(i, _):
            for yc in range(4):
                work(i * (CX - 1), yc)
            return 0

        def middle(x, _):
            work(x, 0)
            work(x, 3)
            return 0

        lax.fori_loop(0, 2, sides, 0)
        lax.fori_loop(1, CX - 1, middle, 0)

    def core_cells(work):
        def middle(x, _):
            work(x, 1)
            work(x, 2)
            return 0

        lax.fori_loop(1, CX - 1, middle, 0)

    def step1(x, yc):
        collided(pad1, [pop[d, x, 8 * yc : 8 * yc + 8, :] for d in range(19)], x, yc)

    def step2(x, yc):
        collided(pad2, [pulled(pad1, d, x, yc) for d in range(19)], x, yc)

    def step3(x, yc):
        f = [pulled(pad2, d, x, yc) for d in range(19)]
        at = slice(8 * yc, 8 * yc + 8)
        for d in range(19):
            new_pop[d, x, at, :] = f[d]
        rho, mom = moments(f)
        inv = 1.0 / rho
        for k in range(3):
            fluid[k, x, at, :] = (mom[k] + 0.5 * forcing[k, x, at, :]) * inv

    loads[5].wait()
    rim(step1)
    halo1 = halo_start(pad1, 0)
    core_cells(step1)
    core_cells(step2)
    halo_finish(pad1, 0, halo1)
    rim(step2)
    halo2 = halo_start(pad2, 1)
    core_cells(step3)
    halo_finish(pad2, 1, halo2)
    rim(step3)

    sampled[...] = dot_nt(fluid[...].reshape(384, NZ).astype(BF16), onehot_z[...])
    for j in range(2):
        samples[j, 192:256, :] = jnp.zeros((64, 128), F32)

    def sample(ka, _):
        for c in range(4):
            for j in range(2):
                cols = slice(256 * c + 128 * j, 256 * c + 128 * j + 128)
                x = sampled[pl.ds(pl.multiple_of(ka * 32, 32), 8), cols]
                for v in range(1, 4):
                    x = jnp.where(inside[j][v], sampled[pl.ds(pl.multiple_of(ka * 32 + 8 * v, 8), 8), cols], x)
                for n, bit in zip((1, 2, 4), bits[j]):
                    x = jnp.where(bit, pltpu.roll(x, 8 - n, 0), x)
                samples[j, pl.ds(ka * 16 + c, 4, stride=4), :] = x[0:4]
        return 0

    lax.fori_loop(0, 12, sample, 0)
    for j in range(2):
        for h in range(2):
            backbuf[:, 2 * j + h, :] = samples[j, 128 * h : 128 * h + 128, :].T
    exchange(backbuf, finbuf, 1)
    exchanged(backbuf, finbuf, 1).wait_recv()

    exchanged(sendbuf, recvbuf, 0).wait_send()
    exchanged(backbuf, finbuf, 1).wait_send()
    for c in halo1 + halo2:
        c.wait_send()


def finish(
    fields, finbuf, weights, take, member,
    fields_hbm, speed_hbm, swim_hbm,
    speed, swim, sem,
):
    stores = [
        pltpu.make_async_copy(source, target, sem.at[i])
        for i, (source, target) in enumerate(((fields, fields_hbm), (speed, speed_hbm), (swim, swim_hbm)))
    ]
    stores[0].start()
    left = iota((8, 128), 1) < 64
    ownpart = own_part()
    back = jnp.concatenate(
        [jnp.concatenate([finbuf[:, 2 * j + h, :] for h in range(2)], axis=1) for j in range(2)], axis=0
    ).astype(BF16)
    cells = dot(take[...], back)
    means = [[], [], []]
    for g in range(6):
        at = slice(8 * g, 8 * g + 8)
        pair, third = cells[at, 0:128], cells[at, 128:256]
        swapped = pltpu.roll(pair, 64, 1)
        each = (jnp.where(left, pair, swapped), jnp.where(left, swapped, pair), jnp.where(left, third, pltpu.roll(third, 64, 1)))
        lhs = jnp.concatenate(
            [jnp.where(ownpart, jnp.concatenate([e] * 4, axis=1), 0.0) for e in each], axis=0
        ).astype(BF16)
        result = 20.0 * dot(lhs, weights[512 * g : 512 * g + 512, :])
        for k in range(3):
            part = result[8 * k : 8 * k + 8]
            speed[k, at, :] = part
            means[k].append(jnp.sum(part, axis=1, keepdims=True) * (1.0 / 128.0))
    stores[1].start()
    belongs = member[...]
    swim[...] = jnp.concatenate(
        [jnp.sum(jnp.concatenate(means[k], axis=0) * belongs, axis=0, keepdims=True) for k in range(3)], axis=0
    )
    stores[2].start()
    for store in stores:
        store.wait()


def body(populations, marker_weights, marker_force, owner_device, stencil_base, block_swimmer):
    vmem = pl.BlockSpec(memory_space=pltpu.VMEM)
    hbm = pl.BlockSpec(memory_space=pl.ANY)
    operands = (
        populations,
        marker_weights.reshape(HELD * 64, 128),
        marker_force.transpose(1, 0, 2),
        owner_device.reshape(1, HELD),
        stencil_base.T,
        block_swimmer.reshape(1, HELD),
    )
    handed = pl.pallas_call(
        kernel,
        out_shape=(
            jax.ShapeDtypeStruct((19, CX, CY, NZ), F32),
            jax.ShapeDtypeStruct((NDEV, 4, 128), F32),
            jax.ShapeDtypeStruct((HELD * 64, 128), BF16),
            jax.ShapeDtypeStruct((HELD, 256), BF16),
            jax.ShapeDtypeStruct((HELD, 4), F32),
        ),
        in_specs=[hbm] * 6,
        out_specs=(vmem,) * 5,
        scratch_shapes=[
            pltpu.VMEM((19, CX, CY, NZ), F32),
            pltpu.VMEM((3, HELD, 128), BF16),
            pltpu.VMEM((1, HELD), jnp.int32),
            pltpu.VMEM((3, HELD), jnp.int32),
            pltpu.VMEM((1, HELD), jnp.int32),
            pltpu.VMEM((NDEV, 4, 128), F32),
            pltpu.VMEM((NDEV, 4, 128), F32),
            pltpu.VMEM((NDEV, 4, 128), F32),
            pltpu.VMEM((2, 256, 128), F32),
            pltpu.VMEM((384, 1024), BF16),
            pltpu.VMEM((384, 1024), BF16),
            pltpu.VMEM((1024, 128), BF16),
            pltpu.VMEM((3, CX, CY, NZ), F32),
            pltpu.VMEM((19, CX + 2, CY + 16, NZ), F32),
            pltpu.VMEM((19, CX + 2, CY + 16, NZ), F32),
            pltpu.VMEM((3, CX, CY, NZ), F32),
            pltpu.VMEM((384, 1024), F32),
            pltpu.VMEM((2, 256, 128), F32),
            pltpu.VMEM((2, 2, 5, 4, 128), F32),
            pltpu.VMEM((2, 2, 5, 4, 128), F32),
            pltpu.VMEM((2, 4, 1, 128), F32),
            pltpu.VMEM((2, 4, 1, 128), F32),
            pltpu.SemaphoreType.DMA((6,)),
            pltpu.SemaphoreType.DMA((2,)),
            pltpu.SemaphoreType.DMA((2,)),
            pltpu.SemaphoreType.DMA((2, 8)),
            pltpu.SemaphoreType.DMA((2, 8)),
        ],
        compiler_params=pltpu.CompilerParams(
            collective_id=0, has_side_effects=True, vmem_limit_bytes=40 * 1024 * 1024
        ),
    )(
        *(pltpu.with_memory_space_constraint(x, pltpu.HBM) for x in operands)
    )
    fields, speed, swim = pl.pallas_call(
        finish,
        out_shape=(
            jax.ShapeDtypeStruct((19, CX, CY, NZ), F32),
            jax.ShapeDtypeStruct((3, HELD, 128), F32),
            jax.ShapeDtypeStruct((3, 4), F32),
        ),
        in_specs=[vmem] * 5,
        out_specs=(hbm,) * 3,
        scratch_shapes=[
            pltpu.VMEM((3, HELD, 128), F32),
            pltpu.VMEM((3, 4), F32),
            pltpu.SemaphoreType.DMA((3,)),
        ],
        compiler_params=pltpu.CompilerParams(vmem_limit_bytes=16 * 1024 * 1024),
    )(*handed)
    return fields, speed.transpose(1, 0, 2), swim


def solution(mesh):
    in_specs = (
        P(None, "gx", "gy", None),
        P(("gx", "gy"), None, None),
        P(("gx", "gy"), None, None),
        P(("gx", "gy"), None),
        P(("gx", "gy"), None),
        P(("gx", "gy")),
    )
    out_specs = (P(None, "gx", "gy", None), P(("gx", "gy"), None, None), P(None, ("gx", "gy")))
    return jax.shard_map(body, mesh=mesh, in_specs=in_specs, out_specs=out_specs, check_vma=False)
```

```python
import jax
import jax.numpy as jnp
from jax import lax
from jax.experimental import pallas as pl
from jax.experimental.pallas import tpu as pltpu
from jax.sharding import PartitionSpec as P

MESH = pl.DeviceIdType.MESH
F32 = jnp.float32
BF16 = jnp.bfloat16

NGX, NGY, NDEV = 16, 8, 128
CX, CY, NZ = 4, 32, 128
HELD = 48
TOP = 8

VEL = (
    (0, 0, 0),
    (1, 0, 0), (-1, 0, 0), (0, 1, 0), (0, -1, 0), (0, 0, 1), (0, 0, -1),
    (1, 1, 0), (-1, -1, 0), (1, -1, 0), (-1, 1, 0),
    (1, 0, 1), (-1, 0, -1), (1, 0, -1), (-1, 0, 1),
    (0, 1, 1), (0, -1, -1), (0, 1, -1), (0, -1, 1),
)
OPP = (0, 2, 1, 4, 3, 6, 5, 8, 7, 10, 9, 12, 11, 14, 13, 16, 15, 18, 17)
WEIGHT = (1.0 / 3.0,) + (1.0 / 18.0,) * 6 + (1.0 / 36.0,) * 12
PAIRS = ((1, 2), (3, 4), (5, 6), (7, 8), (9, 10), (11, 12), (13, 14), (15, 16), (17, 18))

XP = (1, 7, 9, 11, 13)
XM = (2, 8, 10, 12, 14)
REST = (0, 3, 4, 5, 6, 15, 16, 17, 18)
ORDER = XP + XM + REST
AT = {d: i for i, d in enumerate(ORDER)}
YP = (3, 7, 10, 15, 17)
YM = (4, 8, 9, 16, 18)


def iota(shape, dim):
    return lax.broadcasted_iota(jnp.int32, shape, dim)


def dot(a, b):
    return jnp.dot(a, b, preferred_element_type=F32)


def dot_nt(a, b):
    return lax.dot_general(a, b, (((1,), (1,)), ((), ())), preferred_element_type=F32)


def own_part():
    return lax.div(iota((8, 512), 1), 64) == iota((8, 512), 0)


def moments(f):
    rho = f[0]
    mom = [None, None, None]
    for p, m in PAIRS:
        rho = rho + (f[p] + f[m])
        diff = f[p] - f[m]
        for k in range(3):
            if VEL[p][k] == 1:
                mom[k] = diff if mom[k] is None else mom[k] + diff
            elif VEL[p][k] == -1:
                mom[k] = mom[k] - diff
    return rho, mom


def collide(f, force):
    rho, mom = moments(f)
    inv = 1.0 / rho
    u = [(mom[k] + 0.8 * force[k]) * inv for k in range(3)]
    usq = u[0] * u[0] + u[1] * u[1] + u[2] * u[2]
    whole = 1.25 * rho
    calm = 1.0 - 1.5 * usq
    out = [None] * 19
    out[0] = (WEIGHT[0] * whole) * calm - 0.25 * f[0]
    for first, last, w in ((0, 3, 1.0 / 18.0), (3, 9, 1.0 / 36.0)):
        scaled = w * whole
        base = scaled * calm
        linear = 3.0 * scaled
        for p, m in PAIRS[first:last]:
            along = None
            for k in range(3):
                if VEL[p][k] == 1:
                    along = u[k] if along is None else along + u[k]
                elif VEL[p][k] == -1:
                    along = along - u[k]
            turn = linear * along
            even = base + 1.5 * (turn * along)
            out[p] = (even + turn) - 0.25 * f[p]
            out[m] = (even - turn) - 0.25 * f[m]
    return out


def kernel(
    pop_hbm, weights_hbm, force_hbm, owner_hbm, base_hbm, swimmer_hbm,
    new_pop, finbuf, weights, take_out, member_out,
    pop, force, owner, base, swimmer,
    sendbuf, recvbuf, backbuf, turned, spread_hi, spread_lo, onehot_z, forcing, pad1, pad2, fluid, sampled, samples,
    ysend, yrecv, csend, crecv,
    load_sem, send_sem, recv_sem, halo_send, halo_recv,
):
    loads = [
        pltpu.make_async_copy(source, target, load_sem.at[i])
        for i, (source, target) in enumerate(
            ((owner_hbm, owner), (base_hbm, base), (force_hbm, force), (weights_hbm, weights), (swimmer_hbm, swimmer), (pop_hbm, pop))
        )
    ]
    gx, gy = lax.axis_index("gx"), lax.axis_index("gy")
    me = gx * NGY + gy
    core, my_x = lax.rem(gx, 2), lax.rem(lax.div(gx, 2), 4)
    my_y, my_z = lax.div(gy, 2), lax.div(gx, 8) * 2 + lax.rem(gy, 2)

    along_x = [lax.rem(my_x + d, 4) * 2 for d in (1, 3, 2, 0)]

    def to_all(act):
        def offset(digit):
            return jnp.where(digit < 2, 2 * digit + 1, 6 - 2 * digit)

        def step(i, _):
            z = lax.rem(my_z + offset(lax.div(i, 4)), 4)
            tx = lax.div(z, 2) * 8
            ty = lax.rem(my_y + offset(lax.rem(i, 4)), 4) * 2 + lax.rem(z, 2)
            for x in along_x:
                act(tx + x, ty)
                act(tx + x + 1, ty)
            return 0

        lax.fori_loop(0, 15, step, 0)
        first = lax.div(gx, 8) * 8
        for x in along_x[:3]:
            act(first + x, gy)
            act(first + x + 1, gy)
        act(gx + 1 - 2 * core, gy)

    barrier = pltpu.get_barrier_semaphore()
    to_all(lambda tx, ty: pl.semaphore_signal(barrier, inc=1, device_id=(tx, ty), device_id_type=MESH))

    for load in loads:
        load.start()

    for load in loads[:4]:
        load.wait()
    square = (HELD, HELD)
    down, across = iota(square, 0), iota(square, 1)

    def standing(line):
        return jnp.sum(jnp.where(down == across, line, 0), axis=1, keepdims=True)

    row = owner[...]
    col = standing(row)
    same = col == row
    rank_col = jnp.sum(jnp.where(same & (across < down), 1, 0), axis=1, keepdims=True)
    rank_row = jnp.sum(jnp.where(same & (down < across), 1, 0), axis=0, keepdims=True)
    slot_row = rank_row * NDEV + row
    slot_col = rank_col * NDEV + col

    take_out[...] = jnp.where(iota((HELD, 256), 1) == slot_col, 1.0, 0.0).astype(BF16)
    loads[4].wait()
    member_out[...] = jnp.where(lax.rem(standing(swimmer[...]), 4) == iota((HELD, 4), 1), 1.0, 0.0)

    lane = iota((8, 128), 1)
    left = lane < 64
    ownpart = own_part()
    pulls = [force[k].astype(F32) for k in range(3)]
    strip = standing(base[1:2, :]).astype(F32)
    column = standing(base[2:3, :]).astype(F32)
    rows01, rows2x = [], []
    for g in range(6):
        at = slice(8 * g, 8 * g + 8)
        lhs = jnp.concatenate([pulls[k][at] for k in range(3)], axis=0).astype(BF16)
        full = dot_nt(lhs, weights[512 * g : 512 * g + 512, :])
        part = []
        for k in range(3):
            x = jnp.where(ownpart, full[8 * k : 8 * k + 8], 0.0)
            y = (x[:, 0:128] + x[:, 128:256]) + (x[:, 256:384] + x[:, 384:512])
            part.append(y + pltpu.roll(y, 64, 1))
        extra = jnp.where(lane == 64, strip[at], jnp.where(lane == 65, column[at], 0.0))
        rows01.append(jnp.where(left, part[0], part[1]))
        rows2x.append(jnp.where(left, part[2], extra))
    patch = jnp.concatenate([jnp.concatenate(rows01, axis=0), jnp.concatenate(rows2x, axis=0)], axis=1)
    patch_hi = patch.astype(BF16)
    patch_lo = (patch - patch_hi.astype(F32)).astype(BF16)
    put = jnp.where(iota((256, HELD), 0) == slot_row, 1.0, 0.0).astype(BF16)
    outgoing = dot(put, patch_hi) + dot(put, patch_lo)
    for j in range(2):
        for h in range(2):
            sendbuf[:, 2 * j + h, :] = outgoing[128 * j : 128 * j + 128, 128 * h : 128 * h + 128]

    pl.semaphore_wait(barrier, NDEV - 1)

    def exchange(source, target, n):
        to_all(
            lambda tx, ty: pltpu.make_async_remote_copy(
                source.at[tx * NGY + ty], target.at[me], send_sem.at[n], recv_sem.at[n],
                device_id=(tx, ty), device_id_type=MESH,
            ).start()
        )
        target[me] = source[me]

    def exchanged(source, target, n):
        return pltpu.make_async_remote_copy(
            source.at[pl.ds(0, NDEV - 1)], target.at[pl.ds(0, NDEV - 1)], send_sem.at[n], recv_sem.at[n],
            device_id=(lax.rem(gx + 1, NGX), gy), device_id_type=MESH,
        )

    exchange(sendbuf, recvbuf, 0)
    exchanged(sendbuf, recvbuf, 0).wait_recv()

    wide = iota((128, 128), 1)
    for j in range(2):
        for h in range(2):
            got = recvbuf[:, 2 * j + h, :]
            turned[j, 128 * h : 128 * h + 128, :] = got.T
            if h == 1:
                ahead = wide - jnp.broadcast_to(got[:, 65:66], (128, 128)).astype(jnp.int32)
                for c in range(4):
                    onehot_z[256 * c + 128 * j : 256 * c + 128 * j + 128, :] = jnp.where(
                        ahead == c, 1.0, 0.0
                    ).astype(BF16)
    sub = iota((8, 128), 0)
    bits, inside = [], []
    for j in range(2):
        y_first = jnp.broadcast_to(turned[j, 192:193, :].astype(jnp.int32), (8, 128))
        bits.append([(y_first & n) != 0 for n in (1, 2, 4)])
        offs = [sub + 8 * v - y_first for v in range(4)]
        inside.append([(off >= 0) & (off < 4) for off in offs])

    def place(ka):
        rows = slice(32 * ka, 32 * ka + 32)
        for c in range(4):
            for j in range(2):
                x = turned[j, pl.ds(ka * 16 + c, 8, stride=4), :]
                for n, bit in zip((1, 2, 4), bits[j]):
                    x = jnp.where(bit, pltpu.roll(x, n, 0), x)
                hi = x.astype(BF16).astype(F32)
                lo = x - hi
                start = 256 * c + 128 * j
                for piece, ref in ((hi, spread_hi), (lo, spread_lo)):
                    ref[rows, start : start + 128] = jnp.concatenate(
                        [jnp.where(inside[j][v], piece, 0.0) for v in range(4)], axis=0
                    ).astype(BF16)

    for k in range(3):
        for a in range(CX):
            place(CX * k + a)
        rows = slice(128 * k, 128 * k + 128)
        forcing[k] = (dot(spread_hi[rows, :], onehot_z[...]) + dot(spread_lo[rows, :], onehot_z[...])).reshape(CX, CY, NZ)

    east, west = (lax.rem(gx + 1, NGX), gy), (lax.rem(gx + NGX - 1, NGX), gy)
    up, down_ = lax.rem(gy + 1, NGY), lax.rem(gy + NGY - 1, NGY)
    north, south = (gx, up), (gx, down_)
    corners = ((7, (east[0], up)), (8, (west[0], down_)), (9, (east[0], down_)), (10, (west[0], up)))

    zlane = iota((8, NZ), 1)
    ysub = iota((8, NZ), 0)
    at_low, at_high = gy == 0, gy == NGY - 1

    def pulled(pad, d, x, yc):
        ex, ey, ez = VEL[d]
        value = pad[AT[d], x + 1 - ex, TOP + 8 * yc - ey : TOP + 8 * yc - ey + 8, :]
        wall = []
        if ez:
            value = pltpu.roll(value, 1 if ez == 1 else NZ - 1, 1)
            wall.append(zlane == (0 if ez == 1 else NZ - 1))
        if ey == 1 and yc == 0:
            wall.append((ysub == 0) & at_low)
        if ey == -1 and yc == 3:
            wall.append((ysub == 7) & at_high)
        if wall:
            mask = wall[0] if len(wall) == 1 else wall[0] | wall[1]
            value = jnp.where(mask, pad[AT[OPP[d]], x + 1, TOP + 8 * yc : TOP + 8 * yc + 8, :], value)
        return value

    def collided(pad, f, x, yc):
        at = slice(8 * yc, 8 * yc + 8)
        out = collide(f, [forcing[k, x, at, :] for k in range(3)])
        for d in range(19):
            pad[AT[d], x + 1, TOP + 8 * yc : TOP + 8 * yc + 8, :] = out[d]

    def halo_start(pad, n):
        def copy(source, target, i, device):
            c = pltpu.make_async_remote_copy(
                source, target, halo_send.at[n, i], halo_recv.at[n, i], device_id=device, device_id_type=MESH
            )
            c.start()
            return c

        rows = pl.ds(TOP, CY)
        copies = []
        for i, (d, device) in enumerate(corners):
            x = CX if VEL[d][0] == 1 else 1
            y = TOP + CY - 1 if VEL[d][1] == 1 else TOP
            csend[n, i] = pad[AT[d], x, y : y + 1, :]
            copies.append(copy(csend.at[n, i], crecv.at[n, i], 4 + i, device))
        copies.append(copy(pad.at[0:5, CX, rows, :], pad.at[0:5, 0, rows, :], 0, east))
        copies.append(copy(pad.at[5:10, 1, rows, :], pad.at[5:10, CX + 1, rows, :], 1, west))
        for side, dirs, edge, device in ((0, YP, TOP + CY - 1, north), (1, YM, TOP, south)):
            for i, d in enumerate(dirs):
                for x in range(CX):
                    ysend[n, side, i, x : x + 1, :] = pad[AT[d], x + 1, edge : edge + 1, :]
            copies.append(copy(ysend.at[n, side], yrecv.at[n, side], 2 + side, device))
        return copies

    def halo_finish(pad, n, copies):
        for c in copies:
            c.wait_recv()
        for side, dirs, edge in ((0, YP, TOP - 1), (1, YM, TOP + CY)):
            for i, d in enumerate(dirs):
                for x in range(CX):
                    pad[AT[d], x + 1, edge : edge + 1, :] = yrecv[n, side, i, x : x + 1, :]
        for i, (d, device) in enumerate(corners):
            x = 0 if VEL[d][0] == 1 else CX + 1
            y = TOP - 1 if VEL[d][1] == 1 else TOP + CY
            pad[AT[d], x, y : y + 1, :] = crecv[n, i]

    def rim(work):
        def sides(i, _):
            for yc in range(4):
                work(i * (CX - 1), yc)
            return 0

        def middle(x, _):
            work(x, 0)
            work(x, 3)
            return 0

        lax.fori_loop(0, 2, sides, 0)
        lax.fori_loop(1, CX - 1, middle, 0)

    def core_cells(work):
        def middle(x, _):
            work(x, 1)
            work(x, 2)
            return 0

        lax.fori_loop(1, CX - 1, middle, 0)

    def step1(x, yc):
        collided(pad1, [pop[d, x, 8 * yc : 8 * yc + 8, :] for d in range(19)], x, yc)

    def step2(x, yc):
        collided(pad2, [pulled(pad1, d, x, yc) for d in range(19)], x, yc)

    def step3(x, yc):
        f = [pulled(pad2, d, x, yc) for d in range(19)]
        at = slice(8 * yc, 8 * yc + 8)
        for d in range(19):
            new_pop[d, x, at, :] = f[d]
        rho, mom = moments(f)
        inv = 1.0 / rho
        for k in range(3):
            fluid[k, x, at, :] = (mom[k] + 0.5 * forcing[k, x, at, :]) * inv

    loads[5].wait()
    rim(step1)
    halo1 = halo_start(pad1, 0)
    core_cells(step1)
    core_cells(step2)
    halo_finish(pad1, 0, halo1)
    rim(step2)
    halo2 = halo_start(pad2, 1)
    core_cells(step3)
    halo_finish(pad2, 1, halo2)
    rim(step3)

    for j in range(2):
        samples[j, 192:256, :] = jnp.zeros((64, 128), F32)

    def sample(ka):
        for c in range(4):
            for j in range(2):
                cols = slice(256 * c + 128 * j, 256 * c + 128 * j + 128)
                x = sampled[slice(32 * ka, 32 * ka + 8), cols]
                for v in range(1, 4):
                    x = jnp.where(inside[j][v], sampled[slice(32 * ka + 8 * v, 32 * ka + 8 * v + 8), cols], x)
                for n, bit in zip((1, 2, 4), bits[j]):
                    x = jnp.where(bit, pltpu.roll(x, 8 - n, 0), x)
                samples[j, pl.ds(ka * 16 + c, 4, stride=4), :] = x[0:4]

    for k in range(3):
        sampled[128 * k : 128 * k + 128, :] = dot_nt(fluid[k].reshape(128, NZ).astype(BF16), onehot_z[...])
        for a in range(CX):
            sample(CX * k + a)
    for j in range(2):
        for h in range(2):
            backbuf[:, 2 * j + h, :] = samples[j, 128 * h : 128 * h + 128, :].T
    exchange(backbuf, finbuf, 1)
    exchanged(backbuf, finbuf, 1).wait_recv()

    exchanged(sendbuf, recvbuf, 0).wait_send()
    exchanged(backbuf, finbuf, 1).wait_send()
    for c in halo1 + halo2:
        c.wait_send()


def finish(
    fields, finbuf, weights, take, member,
    fields_hbm, speed_hbm, swim_hbm,
    speed, swim, sem,
):
    stores = [
        pltpu.make_async_copy(source, target, sem.at[i])
        for i, (source, target) in enumerate(((fields, fields_hbm), (speed, speed_hbm), (swim, swim_hbm)))
    ]
    stores[0].start()
    left = iota((8, 128), 1) < 64
    ownpart = own_part()
    back = jnp.concatenate(
        [jnp.concatenate([finbuf[:, 2 * j + h, :] for h in range(2)], axis=1) for j in range(2)], axis=0
    ).astype(BF16)
    cells = dot(take[...], back)
    means = [[], [], []]
    for g in range(6):
        at = slice(8 * g, 8 * g + 8)
        pair, third = cells[at, 0:128], cells[at, 128:256]
        swapped = pltpu.roll(pair, 64, 1)
        each = (jnp.where(left, pair, swapped), jnp.where(left, swapped, pair), jnp.where(left, third, pltpu.roll(third, 64, 1)))
        lhs = jnp.concatenate(
            [jnp.where(ownpart, jnp.concatenate([e] * 4, axis=1), 0.0) for e in each], axis=0
        ).astype(BF16)
        result = 20.0 * dot(lhs, weights[512 * g : 512 * g + 512, :])
        for k in range(3):
            part = result[8 * k : 8 * k + 8]
            speed[k, at, :] = part
            means[k].append(jnp.sum(part, axis=1, keepdims=True) * (1.0 / 128.0))
    stores[1].start()
    belongs = member[...]
    swim[...] = jnp.concatenate(
        [jnp.sum(jnp.concatenate(means[k], axis=0) * belongs, axis=0, keepdims=True) for k in range(3)], axis=0
    )
    stores[2].start()
    for store in stores:
        store.wait()


def body(populations, marker_weights, marker_force, owner_device, stencil_base, block_swimmer):
    vmem = pl.BlockSpec(memory_space=pltpu.VMEM)
    hbm = pl.BlockSpec(memory_space=pl.ANY)
    operands = (
        populations,
        marker_weights.reshape(HELD * 64, 128),
        marker_force.transpose(1, 0, 2),
        owner_device.reshape(1, HELD),
        stencil_base.T,
        block_swimmer.reshape(1, HELD),
    )
    handed = pl.pallas_call(
        kernel,
        out_shape=(
            jax.ShapeDtypeStruct((19, CX, CY, NZ), F32),
            jax.ShapeDtypeStruct((NDEV, 4, 128), F32),
            jax.ShapeDtypeStruct((HELD * 64, 128), BF16),
            jax.ShapeDtypeStruct((HELD, 256), BF16),
            jax.ShapeDtypeStruct((HELD, 4), F32),
        ),
        in_specs=[hbm] * 6,
        out_specs=(vmem,) * 5,
        scratch_shapes=[
            pltpu.VMEM((19, CX, CY, NZ), F32),
            pltpu.VMEM((3, HELD, 128), BF16),
            pltpu.VMEM((1, HELD), jnp.int32),
            pltpu.VMEM((3, HELD), jnp.int32),
            pltpu.VMEM((1, HELD), jnp.int32),
            pltpu.VMEM((NDEV, 4, 128), F32),
            pltpu.VMEM((NDEV, 4, 128), F32),
            pltpu.VMEM((NDEV, 4, 128), F32),
            pltpu.VMEM((2, 256, 128), F32),
            pltpu.VMEM((384, 1024), BF16),
            pltpu.VMEM((384, 1024), BF16),
            pltpu.VMEM((1024, 128), BF16),
            pltpu.VMEM((3, CX, CY, NZ), F32),
            pltpu.VMEM((19, CX + 2, CY + 16, NZ), F32),
            pltpu.VMEM((19, CX + 2, CY + 16, NZ), F32),
            pltpu.VMEM((3, CX, CY, NZ), F32),
            pltpu.VMEM((384, 1024), F32),
            pltpu.VMEM((2, 256, 128), F32),
            pltpu.VMEM((2, 2, 5, 4, 128), F32),
            pltpu.VMEM((2, 2, 5, 4, 128), F32),
            pltpu.VMEM((2, 4, 1, 128), F32),
            pltpu.VMEM((2, 4, 1, 128), F32),
            pltpu.SemaphoreType.DMA((6,)),
            pltpu.SemaphoreType.DMA((2,)),
            pltpu.SemaphoreType.DMA((2,)),
            pltpu.SemaphoreType.DMA((2, 8)),
            pltpu.SemaphoreType.DMA((2, 8)),
        ],
        compiler_params=pltpu.CompilerParams(
            collective_id=0, has_side_effects=True, vmem_limit_bytes=40 * 1024 * 1024
        ),
    )(
        *(pltpu.with_memory_space_constraint(x, pltpu.HBM) for x in operands)
    )
    fields, speed, swim = pl.pallas_call(
        finish,
        out_shape=(
            jax.ShapeDtypeStruct((19, CX, CY, NZ), F32),
            jax.ShapeDtypeStruct((3, HELD, 128), F32),
            jax.ShapeDtypeStruct((3, 4), F32),
        ),
        in_specs=[vmem] * 5,
        out_specs=(hbm,) * 3,
        scratch_shapes=[
            pltpu.VMEM((3, HELD, 128), F32),
            pltpu.VMEM((3, 4), F32),
            pltpu.SemaphoreType.DMA((3,)),
        ],
        compiler_params=pltpu.CompilerParams(vmem_limit_bytes=16 * 1024 * 1024),
    )(*handed)
    return fields, speed.transpose(1, 0, 2), swim


def solution(mesh):
    in_specs = (
        P(None, "gx", "gy", None),
        P(("gx", "gy"), None, None),
        P(("gx", "gy"), None, None),
        P(("gx", "gy"), None),
        P(("gx", "gy"), None),
        P(("gx", "gy")),
    )
    out_specs = (P(None, "gx", "gy", None), P(("gx", "gy"), None, None), P(None, ("gx", "gy")))
    return jax.shard_map(body, mesh=mesh, in_specs=in_specs, out_specs=out_specs, check_vma=False)
```

```python
import jax
import jax.numpy as jnp
from jax import lax
from jax.experimental import pallas as pl
from jax.experimental.pallas import tpu as pltpu
from jax.sharding import PartitionSpec as P

MESH = pl.DeviceIdType.MESH
F32 = jnp.float32
BF16 = jnp.bfloat16

NGX, NGY, NDEV = 16, 8, 128
CX, CY, NZ = 4, 32, 128
HELD = 48
TOP = 8

VEL = (
    (0, 0, 0),
    (1, 0, 0), (-1, 0, 0), (0, 1, 0), (0, -1, 0), (0, 0, 1), (0, 0, -1),
    (1, 1, 0), (-1, -1, 0), (1, -1, 0), (-1, 1, 0),
    (1, 0, 1), (-1, 0, -1), (1, 0, -1), (-1, 0, 1),
    (0, 1, 1), (0, -1, -1), (0, 1, -1), (0, -1, 1),
)
OPP = (0, 2, 1, 4, 3, 6, 5, 8, 7, 10, 9, 12, 11, 14, 13, 16, 15, 18, 17)
WEIGHT = (1.0 / 3.0,) + (1.0 / 18.0,) * 6 + (1.0 / 36.0,) * 12
PAIRS = ((1, 2), (3, 4), (5, 6), (7, 8), (9, 10), (11, 12), (13, 14), (15, 16), (17, 18))

XP = (1, 7, 9, 11, 13)
XM = (2, 8, 10, 12, 14)
REST = (0, 3, 4, 5, 6, 15, 16, 17, 18)
ORDER = XP + XM + REST
AT = {d: i for i, d in enumerate(ORDER)}
YP = (3, 7, 10, 15, 17)
YM = (4, 8, 9, 16, 18)


def iota(shape, dim):
    return lax.broadcasted_iota(jnp.int32, shape, dim)


def dot(a, b):
    return jnp.dot(a, b, preferred_element_type=F32)


def dot_nt(a, b):
    return lax.dot_general(a, b, (((1,), (1,)), ((), ())), preferred_element_type=F32)


def own_part():
    return lax.div(iota((8, 512), 1), 64) == iota((8, 512), 0)


def moments(f):
    rho = f[0]
    mom = [None, None, None]
    for p, m in PAIRS:
        rho = rho + (f[p] + f[m])
        diff = f[p] - f[m]
        for k in range(3):
            if VEL[p][k] == 1:
                mom[k] = diff if mom[k] is None else mom[k] + diff
            elif VEL[p][k] == -1:
                mom[k] = mom[k] - diff
    return rho, mom


def collide(f, force):
    rho, mom = moments(f)
    inv = 1.0 / rho
    u = [(mom[k] + 0.8 * force[k]) * inv for k in range(3)]
    usq = u[0] * u[0] + u[1] * u[1] + u[2] * u[2]
    whole = 1.25 * rho
    calm = 1.0 - 1.5 * usq
    out = [None] * 19
    out[0] = (WEIGHT[0] * whole) * calm - 0.25 * f[0]
    for first, last, w in ((0, 3, 1.0 / 18.0), (3, 9, 1.0 / 36.0)):
        scaled = w * whole
        base = scaled * calm
        linear = 3.0 * scaled
        for p, m in PAIRS[first:last]:
            along = None
            for k in range(3):
                if VEL[p][k] == 1:
                    along = u[k] if along is None else along + u[k]
                elif VEL[p][k] == -1:
                    along = along - u[k]
            turn = linear * along
            even = base + 1.5 * (turn * along)
            out[p] = (even + turn) - 0.25 * f[p]
            out[m] = (even - turn) - 0.25 * f[m]
    return out


def kernel(
    pop_hbm, weights_hbm, force_hbm, owner_hbm, base_hbm, swimmer_hbm,
    new_pop, finbuf, weights, take_out, member_out,
    pop, force, owner, base, swimmer,
    sendbuf, recvbuf, backbuf, turned, spread, onehot_z, forcing, pad1, pad2, fluid, sampled, samples,
    ysend, yrecv, csend, crecv,
    load_sem, send_sem, recv_sem, halo_send, halo_recv,
):
    loads = [
        pltpu.make_async_copy(source, target, load_sem.at[i])
        for i, (source, target) in enumerate(
            ((owner_hbm, owner), (base_hbm, base), (force_hbm, force), (weights_hbm, weights), (swimmer_hbm, swimmer), (pop_hbm, pop))
        )
    ]
    gx, gy = lax.axis_index("gx"), lax.axis_index("gy")
    me = gx * NGY + gy
    core, my_x = lax.rem(gx, 2), lax.rem(lax.div(gx, 2), 4)
    my_y, my_z = lax.div(gy, 2), lax.div(gx, 8) * 2 + lax.rem(gy, 2)

    along_x = [lax.rem(my_x + d, 4) * 2 for d in (1, 3, 2, 0)]

    def to_all(act, far=False):
        def offset(digit):
            if far:
                return jnp.where(digit < 2, 2 - digit, lax.rem(digit + 1, 4))
            return jnp.where(digit < 2, 2 * digit + 1, 6 - 2 * digit)

        def step(i, _):
            z = lax.rem(my_z + offset(lax.div(i, 4)), 4)
            tx = lax.div(z, 2) * 8
            ty = lax.rem(my_y + offset(lax.rem(i, 4)), 4) * 2 + lax.rem(z, 2)
            for x in along_x:
                act(tx + x, ty)
                act(tx + x + 1, ty)
            return 0

        lax.fori_loop(0, 15, step, 0)
        first = lax.div(gx, 8) * 8
        for x in along_x[:3]:
            act(first + x, gy)
            act(first + x + 1, gy)
        act(gx + 1 - 2 * core, gy)

    barrier = pltpu.get_barrier_semaphore()
    to_all(lambda tx, ty: pl.semaphore_signal(barrier, inc=1, device_id=(tx, ty), device_id_type=MESH), far=True)

    for load in loads:
        load.start()

    for load in loads[:4]:
        load.wait()
    square = (HELD, HELD)
    down, across = iota(square, 0), iota(square, 1)

    def standing(line):
        return jnp.sum(jnp.where(down == across, line, 0), axis=1, keepdims=True)

    row = owner[...]
    col = standing(row)
    same = col == row
    rank_col = jnp.sum(jnp.where(same & (across < down), 1, 0), axis=1, keepdims=True)
    rank_row = jnp.sum(jnp.where(same & (down < across), 1, 0), axis=0, keepdims=True)
    slot_row = rank_row * NDEV + row
    slot_col = rank_col * NDEV + col

    take_out[...] = jnp.where(iota((HELD, 256), 1) == slot_col, 1.0, 0.0).astype(BF16)
    loads[4].wait()
    member_out[...] = jnp.where(lax.rem(standing(swimmer[...]), 4) == iota((HELD, 4), 1), 1.0, 0.0)

    lane = iota((8, 128), 1)
    left = lane < 64
    ownpart = own_part()
    pulls = [force[k].astype(F32) for k in range(3)]
    strip = standing(base[1:2, :]).astype(F32)
    column = standing(base[2:3, :]).astype(F32)
    rows01, rows2x = [], []
    for g in range(6):
        at = slice(8 * g, 8 * g + 8)
        lhs = jnp.concatenate([pulls[k][at] for k in range(3)], axis=0).astype(BF16)
        full = dot_nt(lhs, weights[512 * g : 512 * g + 512, :])
        part = []
        for k in range(3):
            x = jnp.where(ownpart, full[8 * k : 8 * k + 8], 0.0)
            y = (x[:, 0:128] + x[:, 128:256]) + (x[:, 256:384] + x[:, 384:512])
            part.append(y + pltpu.roll(y, 64, 1))
        extra = jnp.where(lane == 64, strip[at], jnp.where(lane == 65, column[at], 0.0))
        rows01.append(jnp.where(left, part[0], part[1]))
        rows2x.append(jnp.where(left, part[2], extra))
    patch = jnp.concatenate([jnp.concatenate(rows01, axis=0), jnp.concatenate(rows2x, axis=0)], axis=1)
    patch_hi = patch.astype(BF16)
    patch_lo = (patch - patch_hi.astype(F32)).astype(BF16)
    put = jnp.where(iota((256, HELD), 0) == slot_row, 1.0, 0.0).astype(BF16)
    outgoing = dot(put, patch_hi) + dot(put, patch_lo)
    for j in range(2):
        for h in range(2):
            sendbuf[:, 2 * j + h, :] = outgoing[128 * j : 128 * j + 128, 128 * h : 128 * h + 128]

    pl.semaphore_wait(barrier, NDEV - 1)

    def exchange(source, target, n):
        to_all(
            lambda tx, ty: pltpu.make_async_remote_copy(
                source.at[tx * NGY + ty], target.at[me], send_sem.at[n], recv_sem.at[n],
                device_id=(tx, ty), device_id_type=MESH,
            ).start()
        )
        target[me] = source[me]

    def exchanged(source, target, n):
        return pltpu.make_async_remote_copy(
            source.at[pl.ds(0, NDEV - 1)], target.at[pl.ds(0, NDEV - 1)], send_sem.at[n], recv_sem.at[n],
            device_id=(lax.rem(gx + 1, NGX), gy), device_id_type=MESH,
        )

    exchange(sendbuf, recvbuf, 0)
    exchanged(sendbuf, recvbuf, 0).wait_recv()

    wide = iota((128, 128), 1)
    for j in range(2):
        for h in range(2):
            got = recvbuf[:, 2 * j + h, :]
            turned[j, 128 * h : 128 * h + 128, :] = got.T
            if h == 1:
                ahead = wide - jnp.broadcast_to(got[:, 65:66], (128, 128)).astype(jnp.int32)
                for c in range(4):
                    onehot_z[256 * c + 128 * j : 256 * c + 128 * j + 128, :] = jnp.where(
                        ahead == c, 1.0, 0.0
                    ).astype(BF16)
    sub = iota((8, 128), 0)
    bits, inside = [], []
    for j in range(2):
        y_first = jnp.broadcast_to(turned[j, 192:193, :].astype(jnp.int32), (8, 128))
        bits.append([(y_first & n) != 0 for n in (1, 2, 4)])
        offs = [sub + 8 * v - y_first for v in range(4)]
        inside.append([(off >= 0) & (off < 4) for off in offs])

    def place(k, a):
        ka = CX * k + a
        for c in range(4):
            for j in range(2):
                x = turned[j, pl.ds(ka * 16 + c, 8, stride=4), :]
                for n, bit in zip((1, 2, 4), bits[j]):
                    x = jnp.where(bit, pltpu.roll(x, n, 0), x)
                hi = x.astype(BF16).astype(F32)
                lo = x - hi
                start = 256 * c + 128 * j
                for piece, rows in ((hi, slice(32 * a, 32 * a + 32)), (lo, slice(128 + 32 * a, 160 + 32 * a))):
                    spread[k, rows, start : start + 128] = jnp.concatenate(
                        [jnp.where(inside[j][v], piece, 0.0) for v in range(4)], axis=0
                    ).astype(BF16)

    for k in range(3):
        for a in range(CX):
            place(k, a)
        both = dot(spread[k], onehot_z[...])
        forcing[k] = (both[:128] + both[128:]).reshape(CX, CY, NZ)

    east, west = (lax.rem(gx + 1, NGX), gy), (lax.rem(gx + NGX - 1, NGX), gy)
    up, down_ = lax.rem(gy + 1, NGY), lax.rem(gy + NGY - 1, NGY)
    north, south = (gx, up), (gx, down_)
    corners = ((7, (east[0], up)), (8, (west[0], down_)), (9, (east[0], down_)), (10, (west[0], up)))

    zlane = iota((8, NZ), 1)
    ysub = iota((8, NZ), 0)
    at_low, at_high = gy == 0, gy == NGY - 1

    def pulled(pad, d, x, yc):
        ex, ey, ez = VEL[d]
        value = pad[AT[d], x + 1 - ex, TOP + 8 * yc - ey : TOP + 8 * yc - ey + 8, :]
        wall = []
        if ez:
            value = pltpu.roll(value, 1 if ez == 1 else NZ - 1, 1)
            wall.append(zlane == (0 if ez == 1 else NZ - 1))
        if ey == 1 and yc == 0:
            wall.append((ysub == 0) & at_low)
        if ey == -1 and yc == 3:
            wall.append((ysub == 7) & at_high)
        if wall:
            mask = wall[0] if len(wall) == 1 else wall[0] | wall[1]
            value = jnp.where(mask, pad[AT[OPP[d]], x + 1, TOP + 8 * yc : TOP + 8 * yc + 8, :], value)
        return value

    def collided(pad, f, x, yc):
        at = slice(8 * yc, 8 * yc + 8)
        out = collide(f, [forcing[k, x, at, :] for k in range(3)])
        for d in range(19):
            pad[AT[d], x + 1, TOP + 8 * yc : TOP + 8 * yc + 8, :] = out[d]

    def halo_copy(source, target, n, i, device):
        c = pltpu.make_async_remote_copy(
            source, target, halo_send.at[n, i], halo_recv.at[n, i], device_id=device, device_id_type=MESH
        )
        c.start()
        return c

    def send_corners(pad, n):
        copies = []
        for i, (d, device) in enumerate(corners):
            x = CX if VEL[d][0] == 1 else 1
            y = TOP + CY - 1 if VEL[d][1] == 1 else TOP
            csend[n, i] = pad[AT[d], x, y : y + 1, :]
            copies.append(halo_copy(csend.at[n, i], crecv.at[n, i], n, 4 + i, device))
        return copies

    def send_x(pad, n):
        rows = pl.ds(TOP, CY)
        return [
            halo_copy(pad.at[0:5, CX, rows, :], pad.at[0:5, 0, rows, :], n, 0, east),
            halo_copy(pad.at[5:10, 1, rows, :], pad.at[5:10, CX + 1, rows, :], n, 1, west),
        ]

    def send_y(pad, n):
        copies = []
        for side, dirs, edge, device in ((0, YP, TOP + CY - 1, north), (1, YM, TOP, south)):
            for i, d in enumerate(dirs):
                for x in range(CX):
                    ysend[n, side, i, x : x + 1, :] = pad[AT[d], x + 1, edge : edge + 1, :]
            copies.append(halo_copy(ysend.at[n, side], yrecv.at[n, side], n, 2 + side, device))
        return copies

    def halo_finish(pad, n, copies):
        for c in copies:
            c.wait_recv()
        for side, dirs, edge in ((0, YP, TOP - 1), (1, YM, TOP + CY)):
            for i, d in enumerate(dirs):
                for x in range(CX):
                    pad[AT[d], x + 1, edge : edge + 1, :] = yrecv[n, side, i, x : x + 1, :]
        for i, (d, device) in enumerate(corners):
            x = 0 if VEL[d][0] == 1 else CX + 1
            y = TOP - 1 if VEL[d][1] == 1 else TOP + CY
            pad[AT[d], x, y : y + 1, :] = crecv[n, i]

    def cells(work, xs, ycs):
        for x in xs:
            for yc in ycs:
                work(x, yc)

    outer, inner = (0, 3), (1, 2)

    def rim_sent(work, pad, n):
        cells(work, outer, outer)
        copies = send_corners(pad, n)
        cells(work, outer, inner)
        copies += send_x(pad, n)
        cells(work, inner, outer)
        return copies + send_y(pad, n)

    def step1(x, yc):
        collided(pad1, [pop[d, x, 8 * yc : 8 * yc + 8, :] for d in range(19)], x, yc)

    def step2(x, yc):
        collided(pad2, [pulled(pad1, d, x, yc) for d in range(19)], x, yc)

    def step3(x, yc):
        at = slice(8 * yc, 8 * yc + 8)
        rho, mom = moments([pulled(pad2, d, x, yc) for d in range(19)])
        inv = 1.0 / rho
        for k in range(3):
            fluid[k, x, at, :] = (mom[k] + 0.5 * forcing[k, x, at, :]) * inv

    def keep(x, yc):
        for d in range(19):
            new_pop[d, x, 8 * yc : 8 * yc + 8, :] = pulled(pad2, d, x, yc)

    every = range(4)
    loads[5].wait()
    halo1 = rim_sent(step1, pad1, 0)
    cells(step1, inner, inner)
    cells(step2, inner, inner)
    halo_finish(pad1, 0, halo1)
    halo2 = rim_sent(step2, pad2, 1)
    cells(step3, inner, inner)
    halo_finish(pad2, 1, halo2)
    cells(step3, outer, every)
    cells(step3, inner, outer)

    for j in range(2):
        samples[j, 192:256, :] = jnp.zeros((64, 128), F32)

    def sample(ka):
        for c in range(4):
            for j in range(2):
                cols = slice(256 * c + 128 * j, 256 * c + 128 * j + 128)
                x = sampled[slice(32 * ka, 32 * ka + 8), cols]
                for v in range(1, 4):
                    x = jnp.where(inside[j][v], sampled[slice(32 * ka + 8 * v, 32 * ka + 8 * v + 8), cols], x)
                for n, bit in zip((1, 2, 4), bits[j]):
                    x = jnp.where(bit, pltpu.roll(x, 8 - n, 0), x)
                samples[j, pl.ds(ka * 16 + c, 4, stride=4), :] = x[0:4]

    for k in range(3):
        sampled[128 * k : 128 * k + 128, :] = dot_nt(fluid[k].reshape(128, NZ).astype(BF16), onehot_z[...])
        for a in range(CX):
            sample(CX * k + a)
    for j in range(2):
        for h in range(2):
            backbuf[:, 2 * j + h, :] = samples[j, 128 * h : 128 * h + 128, :].T
    exchange(backbuf, finbuf, 1)
    lax.fori_loop(0, CX, lambda x, c: (cells(keep, (x,), every), c)[1], 0)
    exchanged(backbuf, finbuf, 1).wait_recv()

    exchanged(sendbuf, recvbuf, 0).wait_send()
    exchanged(backbuf, finbuf, 1).wait_send()
    for c in halo1 + halo2:
        c.wait_send()


def finish(
    fields, finbuf, weights, take, member,
    fields_hbm, speed_hbm, swim_hbm,
    speed, swim, sem,
):
    stores = [
        pltpu.make_async_copy(source, target, sem.at[i])
        for i, (source, target) in enumerate(((fields, fields_hbm), (speed, speed_hbm), (swim, swim_hbm)))
    ]
    stores[0].start()
    left = iota((8, 128), 1) < 64
    ownpart = own_part()
    back = jnp.concatenate(
        [jnp.concatenate([finbuf[:, 2 * j + h, :] for h in range(2)], axis=1) for j in range(2)], axis=0
    ).astype(BF16)
    cells = dot(take[...], back)
    means = [[], [], []]
    for g in range(6):
        at = slice(8 * g, 8 * g + 8)
        pair, third = cells[at, 0:128], cells[at, 128:256]
        swapped = pltpu.roll(pair, 64, 1)
        each = (jnp.where(left, pair, swapped), jnp.where(left, swapped, pair), jnp.where(left, third, pltpu.roll(third, 64, 1)))
        lhs = jnp.concatenate(
            [jnp.where(ownpart, jnp.concatenate([e] * 4, axis=1), 0.0) for e in each], axis=0
        ).astype(BF16)
        result = 20.0 * dot(lhs, weights[512 * g : 512 * g + 512, :])
        for k in range(3):
            part = result[8 * k : 8 * k + 8]
            speed[k, at, :] = part
            means[k].append(jnp.sum(part, axis=1, keepdims=True) * (1.0 / 128.0))
    stores[1].start()
    belongs = member[...]
    swim[...] = jnp.concatenate(
        [jnp.sum(jnp.concatenate(means[k], axis=0) * belongs, axis=0, keepdims=True) for k in range(3)], axis=0
    )
    stores[2].start()
    for store in stores:
        store.wait()


def body(populations, marker_weights, marker_force, owner_device, stencil_base, block_swimmer):
    vmem = pl.BlockSpec(memory_space=pltpu.VMEM)
    hbm = pl.BlockSpec(memory_space=pl.ANY)
    operands = (
        populations,
        marker_weights.reshape(HELD * 64, 128),
        marker_force.transpose(1, 0, 2),
        owner_device.reshape(1, HELD),
        stencil_base.T,
        block_swimmer.reshape(1, HELD),
    )
    handed = pl.pallas_call(
        kernel,
        out_shape=(
            jax.ShapeDtypeStruct((19, CX, CY, NZ), F32),
            jax.ShapeDtypeStruct((NDEV, 4, 128), F32),
            jax.ShapeDtypeStruct((HELD * 64, 128), BF16),
            jax.ShapeDtypeStruct((HELD, 256), BF16),
            jax.ShapeDtypeStruct((HELD, 4), F32),
        ),
        in_specs=[hbm] * 6,
        out_specs=(vmem,) * 5,
        scratch_shapes=[
            pltpu.VMEM((19, CX, CY, NZ), F32),
            pltpu.VMEM((3, HELD, 128), BF16),
            pltpu.VMEM((1, HELD), jnp.int32),
            pltpu.VMEM((3, HELD), jnp.int32),
            pltpu.VMEM((1, HELD), jnp.int32),
            pltpu.VMEM((NDEV, 4, 128), F32),
            pltpu.VMEM((NDEV, 4, 128), F32),
            pltpu.VMEM((NDEV, 4, 128), F32),
            pltpu.VMEM((2, 256, 128), F32),
            pltpu.VMEM((3, 256, 1024), BF16),
            pltpu.VMEM((1024, 128), BF16),
            pltpu.VMEM((3, CX, CY, NZ), F32),
            pltpu.VMEM((19, CX + 2, CY + 16, NZ), F32),
            pltpu.VMEM((19, CX + 2, CY + 16, NZ), F32),
            pltpu.VMEM((3, CX, CY, NZ), F32),
            pltpu.VMEM((384, 1024), F32),
            pltpu.VMEM((2, 256, 128), F32),
            pltpu.VMEM((2, 2, 5, 4, 128), F32),
            pltpu.VMEM((2, 2, 5, 4, 128), F32),
            pltpu.VMEM((2, 4, 1, 128), F32),
            pltpu.VMEM((2, 4, 1, 128), F32),
            pltpu.SemaphoreType.DMA((6,)),
            pltpu.SemaphoreType.DMA((2,)),
            pltpu.SemaphoreType.DMA((2,)),
            pltpu.SemaphoreType.DMA((2, 8)),
            pltpu.SemaphoreType.DMA((2, 8)),
        ],
        compiler_params=pltpu.CompilerParams(
            collective_id=0, has_side_effects=True, vmem_limit_bytes=40 * 1024 * 1024
        ),
    )(
        *(pltpu.with_memory_space_constraint(x, pltpu.HBM) for x in operands)
    )
    fields, speed, swim = pl.pallas_call(
        finish,
        out_shape=(
            jax.ShapeDtypeStruct((19, CX, CY, NZ), F32),
            jax.ShapeDtypeStruct((3, HELD, 128), F32),
            jax.ShapeDtypeStruct((3, 4), F32),
        ),
        in_specs=[vmem] * 5,
        out_specs=(hbm,) * 3,
        scratch_shapes=[
            pltpu.VMEM((3, HELD, 128), F32),
            pltpu.VMEM((3, 4), F32),
            pltpu.SemaphoreType.DMA((3,)),
        ],
        compiler_params=pltpu.CompilerParams(vmem_limit_bytes=16 * 1024 * 1024),
    )(*handed)
    return fields, speed.transpose(1, 0, 2), swim


def solution(mesh):
    in_specs = (
        P(None, "gx", "gy", None),
        P(("gx", "gy"), None, None),
        P(("gx", "gy"), None, None),
        P(("gx", "gy"), None),
        P(("gx", "gy"), None),
        P(("gx", "gy")),
    )
    out_specs = (P(None, "gx", "gy", None), P(("gx", "gy"), None, None), P(None, ("gx", "gy")))
    return jax.shard_map(body, mesh=mesh, in_specs=in_specs, out_specs=out_specs, check_vma=False)
```

```python
import jax
import jax.numpy as jnp
from jax import lax
from jax.experimental import pallas as pl
from jax.experimental.pallas import tpu as pltpu
from jax.sharding import PartitionSpec as P

MESH = pl.DeviceIdType.MESH
F32 = jnp.float32
BF16 = jnp.bfloat16

NGX, NGY, NDEV = 16, 8, 128
CX, CY, NZ = 4, 32, 128
HELD = 48
TOP = 8

VEL = (
    (0, 0, 0),
    (1, 0, 0), (-1, 0, 0), (0, 1, 0), (0, -1, 0), (0, 0, 1), (0, 0, -1),
    (1, 1, 0), (-1, -1, 0), (1, -1, 0), (-1, 1, 0),
    (1, 0, 1), (-1, 0, -1), (1, 0, -1), (-1, 0, 1),
    (0, 1, 1), (0, -1, -1), (0, 1, -1), (0, -1, 1),
)
OPP = (0, 2, 1, 4, 3, 6, 5, 8, 7, 10, 9, 12, 11, 14, 13, 16, 15, 18, 17)
WEIGHT = (1.0 / 3.0,) + (1.0 / 18.0,) * 6 + (1.0 / 36.0,) * 12
PAIRS = ((1, 2), (3, 4), (5, 6), (7, 8), (9, 10), (11, 12), (13, 14), (15, 16), (17, 18))

XP = (1, 7, 9, 11, 13)
XM = (2, 8, 10, 12, 14)
REST = (0, 3, 4, 5, 6, 15, 16, 17, 18)
ORDER = XP + XM + REST
AT = {d: i for i, d in enumerate(ORDER)}
YP = (3, 7, 10, 15, 17)
YM = (4, 8, 9, 16, 18)


def iota(shape, dim):
    return lax.broadcasted_iota(jnp.int32, shape, dim)


def dot(a, b):
    return jnp.dot(a, b, preferred_element_type=F32)


def dot_nt(a, b):
    return lax.dot_general(a, b, (((1,), (1,)), ((), ())), preferred_element_type=F32)


def own_part():
    return lax.div(iota((8, 512), 1), 64) == iota((8, 512), 0)


def moments(f):
    rho = f[0]
    mom = [None, None, None]
    for p, m in PAIRS:
        rho = rho + (f[p] + f[m])
        diff = f[p] - f[m]
        for k in range(3):
            if VEL[p][k] == 1:
                mom[k] = diff if mom[k] is None else mom[k] + diff
            elif VEL[p][k] == -1:
                mom[k] = mom[k] - diff
    return rho, mom


def collide(f, force):
    rho, mom = moments(f)
    inv = 1.0 / rho
    u = [(mom[k] + 0.8 * force[k]) * inv for k in range(3)]
    usq = u[0] * u[0] + u[1] * u[1] + u[2] * u[2]
    whole = 1.25 * rho
    calm = 1.0 - 1.5 * usq
    out = [None] * 19
    out[0] = (WEIGHT[0] * whole) * calm - 0.25 * f[0]
    for first, last, w in ((0, 3, 1.0 / 18.0), (3, 9, 1.0 / 36.0)):
        scaled = w * whole
        base = scaled * calm
        linear = 3.0 * scaled
        for p, m in PAIRS[first:last]:
            along = None
            for k in range(3):
                if VEL[p][k] == 1:
                    along = u[k] if along is None else along + u[k]
                elif VEL[p][k] == -1:
                    along = along - u[k]
            turn = linear * along
            even = base + 1.5 * (turn * along)
            out[p] = (even + turn) - 0.25 * f[p]
            out[m] = (even - turn) - 0.25 * f[m]
    return out


def kernel(
    pop_hbm, weights_hbm, force_hbm, owner_hbm, base_hbm, swimmer_hbm,
    new_pop, finbuf, weights, take_out, member_out,
    pop, force, owner, base, swimmer,
    sendbuf, recvbuf, backbuf, turned, spread, onehot_z, forcing, pad1, pad2, fluid, sampled, samples,
    ysend, yrecv, csend, crecv,
    load_sem, send_sem, recv_sem, halo_send, halo_recv,
):
    loads = [
        pltpu.make_async_copy(source, target, load_sem.at[i])
        for i, (source, target) in enumerate(
            ((owner_hbm, owner), (base_hbm, base), (force_hbm, force), (weights_hbm, weights), (swimmer_hbm, swimmer), (pop_hbm, pop))
        )
    ]
    gx, gy = lax.axis_index("gx"), lax.axis_index("gy")
    me = gx * NGY + gy
    core, my_x = lax.rem(gx, 2), lax.rem(lax.div(gx, 2), 4)
    my_y, my_z = lax.div(gy, 2), lax.div(gx, 8) * 2 + lax.rem(gy, 2)

    along_x = [lax.rem(my_x + d, 4) * 2 for d in (1, 3, 2, 0)]

    def to_all(act):
        def offset(digit):
            return jnp.where(digit < 2, 2 - digit, lax.rem(digit + 1, 4))

        def step(i, _):
            z = lax.rem(my_z + offset(lax.div(i, 4)), 4)
            tx = lax.div(z, 2) * 8
            ty = lax.rem(my_y + offset(lax.rem(i, 4)), 4) * 2 + lax.rem(z, 2)
            for x in along_x:
                act(tx + x, ty)
                act(tx + x + 1, ty)
            return 0

        lax.fori_loop(0, 15, step, 0)
        first = lax.div(gx, 8) * 8
        for x in along_x[:3]:
            act(first + x, gy)
            act(first + x + 1, gy)
        act(gx + 1 - 2 * core, gy)

    barrier = pltpu.get_barrier_semaphore()
    to_all(lambda tx, ty: pl.semaphore_signal(barrier, inc=1, device_id=(tx, ty), device_id_type=MESH))

    for load in loads:
        load.start()

    for load in loads[:4]:
        load.wait()
    square = (HELD, HELD)
    down, across = iota(square, 0), iota(square, 1)

    def standing(line):
        return jnp.sum(jnp.where(down == across, line, 0), axis=1, keepdims=True)

    row = owner[...]
    col = standing(row)
    same = col == row
    rank_col = jnp.sum(jnp.where(same & (across < down), 1, 0), axis=1, keepdims=True)
    rank_row = jnp.sum(jnp.where(same & (down < across), 1, 0), axis=0, keepdims=True)
    slot_row = rank_row * NDEV + row
    slot_col = rank_col * NDEV + col

    take_out[...] = jnp.where(iota((HELD, 256), 1) == slot_col, 1.0, 0.0).astype(BF16)
    loads[4].wait()
    member_out[...] = jnp.where(lax.rem(standing(swimmer[...]), 4) == iota((HELD, 4), 1), 1.0, 0.0)

    lane = iota((8, 128), 1)
    left = lane < 64
    ownpart = own_part()
    pulls = [force[k].astype(F32) for k in range(3)]
    strip = standing(base[1:2, :]).astype(F32)
    column = standing(base[2:3, :]).astype(F32)
    rows01, rows2x = [], []
    for g in range(6):
        at = slice(8 * g, 8 * g + 8)
        lhs = jnp.concatenate([pulls[k][at] for k in range(3)], axis=0).astype(BF16)
        full = dot_nt(lhs, weights[512 * g : 512 * g + 512, :])
        part = []
        for k in range(3):
            x = jnp.where(ownpart, full[8 * k : 8 * k + 8], 0.0)
            y = (x[:, 0:128] + x[:, 128:256]) + (x[:, 256:384] + x[:, 384:512])
            part.append(y + pltpu.roll(y, 64, 1))
        extra = jnp.where(lane == 64, strip[at], jnp.where(lane == 65, column[at], 0.0))
        rows01.append(jnp.where(left, part[0], part[1]))
        rows2x.append(jnp.where(left, part[2], extra))
    patch = jnp.concatenate([jnp.concatenate(rows01, axis=0), jnp.concatenate(rows2x, axis=0)], axis=1)
    patch_hi = patch.astype(BF16)
    patch_lo = (patch - patch_hi.astype(F32)).astype(BF16)
    put = jnp.where(iota((256, HELD), 0) == slot_row, 1.0, 0.0).astype(BF16)
    outgoing = dot(put, patch_hi) + dot(put, patch_lo)
    for j in range(2):
        for h in range(2):
            sendbuf[:, 2 * j + h, :] = outgoing[128 * j : 128 * j + 128, 128 * h : 128 * h + 128]

    pl.semaphore_wait(barrier, NDEV - 1)

    def exchange(source, target, n):
        to_all(
            lambda tx, ty: pltpu.make_async_remote_copy(
                source.at[tx * NGY + ty], target.at[me], send_sem.at[n], recv_sem.at[n],
                device_id=(tx, ty), device_id_type=MESH,
            ).start()
        )
        target[me] = source[me]

    def exchanged(source, target, n):
        return pltpu.make_async_remote_copy(
            source.at[pl.ds(0, NDEV - 1)], target.at[pl.ds(0, NDEV - 1)], send_sem.at[n], recv_sem.at[n],
            device_id=(lax.rem(gx + 1, NGX), gy), device_id_type=MESH,
        )

    exchange(sendbuf, recvbuf, 0)
    exchanged(sendbuf, recvbuf, 0).wait_recv()

    wide = iota((128, 128), 1)
    for j in range(2):
        for h in range(2):
            got = recvbuf[:, 2 * j + h, :]
            turned[j, 128 * h : 128 * h + 128, :] = got.T
            if h == 1:
                ahead = wide - jnp.broadcast_to(got[:, 65:66], (128, 128)).astype(jnp.int32)
                for c in range(4):
                    onehot_z[256 * c + 128 * j : 256 * c + 128 * j + 128, :] = jnp.where(
                        ahead == c, 1.0, 0.0
                    ).astype(BF16)
    sub = iota((8, 128), 0)
    bits, inside = [], []
    for j in range(2):
        y_first = jnp.broadcast_to(turned[j, 192:193, :].astype(jnp.int32), (8, 128))
        bits.append([(y_first & n) != 0 for n in (1, 2, 4)])
        offs = [sub + 8 * v - y_first for v in range(4)]
        inside.append([(off >= 0) & (off < 4) for off in offs])

    def place(k, a):
        ka = CX * k + a
        for c in range(4):
            for j in range(2):
                x = turned[j, pl.ds(ka * 16 + c, 8, stride=4), :]
                for n, bit in zip((1, 2, 4), bits[j]):
                    x = jnp.where(bit, pltpu.roll(x, n, 0), x)
                hi = x.astype(BF16).astype(F32)
                lo = x - hi
                start = 256 * c + 128 * j
                for piece, rows in ((hi, slice(32 * a, 32 * a + 32)), (lo, slice(128 + 32 * a, 160 + 32 * a))):
                    spread[k, rows, start : start + 128] = jnp.concatenate(
                        [jnp.where(inside[j][v], piece, 0.0) for v in range(4)], axis=0
                    ).astype(BF16)

    for k in range(3):
        for a in range(CX):
            place(k, a)
        both = dot(spread[k], onehot_z[...])
        forcing[k] = (both[:128] + both[128:]).reshape(CX, CY, NZ)

    east, west = (lax.rem(gx + 1, NGX), gy), (lax.rem(gx + NGX - 1, NGX), gy)
    up, down_ = lax.rem(gy + 1, NGY), lax.rem(gy + NGY - 1, NGY)
    north, south = (gx, up), (gx, down_)
    corners = ((7, (east[0], up)), (8, (west[0], down_)), (9, (east[0], down_)), (10, (west[0], up)))

    zlane = iota((8, NZ), 1)
    ysub = iota((8, NZ), 0)
    at_low, at_high = gy == 0, gy == NGY - 1

    def pulled(pad, d, x, yc):
        ex, ey, ez = VEL[d]
        value = pad[AT[d], x + 1 - ex, TOP + 8 * yc - ey : TOP + 8 * yc - ey + 8, :]
        wall = []
        if ez:
            value = pltpu.roll(value, 1 if ez == 1 else NZ - 1, 1)
            wall.append(zlane == (0 if ez == 1 else NZ - 1))
        if ey == 1 and yc == 0:
            wall.append((ysub == 0) & at_low)
        if ey == -1 and yc == 3:
            wall.append((ysub == 7) & at_high)
        if wall:
            mask = wall[0] if len(wall) == 1 else wall[0] | wall[1]
            value = jnp.where(mask, pad[AT[OPP[d]], x + 1, TOP + 8 * yc : TOP + 8 * yc + 8, :], value)
        return value

    def collided(pad, f, x, yc):
        at = slice(8 * yc, 8 * yc + 8)
        out = collide(f, [forcing[k, x, at, :] for k in range(3)])
        for d in range(19):
            pad[AT[d], x + 1, TOP + 8 * yc : TOP + 8 * yc + 8, :] = out[d]

    def halo_copy(source, target, n, i, device):
        c = pltpu.make_async_remote_copy(
            source, target, halo_send.at[n, i], halo_recv.at[n, i], device_id=device, device_id_type=MESH
        )
        c.start()
        return c

    def send_corners(pad, n):
        copies = []
        for i, (d, device) in enumerate(corners):
            x = CX if VEL[d][0] == 1 else 1
            y = TOP + CY - 1 if VEL[d][1] == 1 else TOP
            csend[n, i] = pad[AT[d], x, y : y + 1, :]
            copies.append(halo_copy(csend.at[n, i], crecv.at[n, i], n, 4 + i, device))
        return copies

    def send_x(pad, n):
        rows = pl.ds(TOP, CY)
        return [
            halo_copy(pad.at[0:5, CX, rows, :], pad.at[0:5, 0, rows, :], n, 0, east),
            halo_copy(pad.at[5:10, 1, rows, :], pad.at[5:10, CX + 1, rows, :], n, 1, west),
        ]

    def send_y(pad, n):
        copies = []
        for side, dirs, edge, device in ((0, YP, TOP + CY - 1, north), (1, YM, TOP, south)):
            for i, d in enumerate(dirs):
                for x in range(CX):
                    ysend[n, side, i, x : x + 1, :] = pad[AT[d], x + 1, edge : edge + 1, :]
            copies.append(halo_copy(ysend.at[n, side], yrecv.at[n, side], n, 2 + side, device))
        return copies

    def halo_finish(pad, n, copies):
        for c in copies:
            c.wait_recv()
        for side, dirs, edge in ((0, YP, TOP - 1), (1, YM, TOP + CY)):
            for i, d in enumerate(dirs):
                for x in range(CX):
                    pad[AT[d], x + 1, edge : edge + 1, :] = yrecv[n, side, i, x : x + 1, :]
        for i, (d, device) in enumerate(corners):
            x = 0 if VEL[d][0] == 1 else CX + 1
            y = TOP - 1 if VEL[d][1] == 1 else TOP + CY
            pad[AT[d], x, y : y + 1, :] = crecv[n, i]

    def cells(work, xs, ycs):
        for x in xs:
            for yc in ycs:
                work(x, yc)

    outer, inner = (0, 3), (1, 2)

    def rim_sent(work, pad, n):
        cells(work, outer, outer)
        copies = send_corners(pad, n)
        cells(work, outer, inner)
        copies += send_x(pad, n)
        cells(work, inner, outer)
        return copies + send_y(pad, n)

    def step1(x, yc):
        collided(pad1, [pop[d, x, 8 * yc : 8 * yc + 8, :] for d in range(19)], x, yc)

    def step2(x, yc):
        collided(pad2, [pulled(pad1, d, x, yc) for d in range(19)], x, yc)

    def step3(x, yc):
        at = slice(8 * yc, 8 * yc + 8)
        rho, mom = moments([pulled(pad2, d, x, yc) for d in range(19)])
        inv = 1.0 / rho
        for k in range(3):
            fluid[k, x, at, :] = (mom[k] + 0.5 * forcing[k, x, at, :]) * inv

    def keep(x, yc):
        for d in range(19):
            new_pop[d, x, 8 * yc : 8 * yc + 8, :] = pulled(pad2, d, x, yc)

    every = range(4)
    loads[5].wait()
    halo1 = rim_sent(step1, pad1, 0)
    cells(step1, inner, inner)
    cells(step2, inner, inner)
    halo_finish(pad1, 0, halo1)
    halo2 = rim_sent(step2, pad2, 1)
    cells(step3, inner, inner)
    halo_finish(pad2, 1, halo2)
    cells(step3, outer, every)
    cells(step3, inner, outer)

    for j in range(2):
        samples[j, 192:256, :] = jnp.zeros((64, 128), F32)

    def sample(ka):
        for c in range(4):
            for j in range(2):
                cols = slice(256 * c + 128 * j, 256 * c + 128 * j + 128)
                x = sampled[slice(32 * ka, 32 * ka + 8), cols]
                for v in range(1, 4):
                    x = jnp.where(inside[j][v], sampled[slice(32 * ka + 8 * v, 32 * ka + 8 * v + 8), cols], x)
                for n, bit in zip((1, 2, 4), bits[j]):
                    x = jnp.where(bit, pltpu.roll(x, 8 - n, 0), x)
                samples[j, pl.ds(ka * 16 + c, 4, stride=4), :] = x[0:4]

    for k in range(3):
        sampled[128 * k : 128 * k + 128, :] = dot_nt(fluid[k].reshape(128, NZ).astype(BF16), onehot_z[...])
        for a in range(CX):
            sample(CX * k + a)
    for j in range(2):
        for h in range(2):
            backbuf[:, 2 * j + h, :] = samples[j, 128 * h : 128 * h + 128, :].T
    exchange(backbuf, finbuf, 1)
    lax.fori_loop(0, CX, lambda x, c: (cells(keep, (x,), every), c)[1], 0)
    exchanged(backbuf, finbuf, 1).wait_recv()

    exchanged(sendbuf, recvbuf, 0).wait_send()
    exchanged(backbuf, finbuf, 1).wait_send()
    for c in halo1 + halo2:
        c.wait_send()


def finish(
    fields, finbuf, weights, take, member,
    fields_hbm, speed_hbm, swim_hbm,
    speed, swim, sem,
):
    stores = [
        pltpu.make_async_copy(source, target, sem.at[i])
        for i, (source, target) in enumerate(((fields, fields_hbm), (speed, speed_hbm), (swim, swim_hbm)))
    ]
    stores[0].start()
    left = iota((8, 128), 1) < 64
    ownpart = own_part()
    back = jnp.concatenate(
        [jnp.concatenate([finbuf[:, 2 * j + h, :] for h in range(2)], axis=1) for j in range(2)], axis=0
    ).astype(BF16)
    cells = dot(take[...], back)
    means = [[], [], []]
    for g in range(6):
        at = slice(8 * g, 8 * g + 8)
        pair, third = cells[at, 0:128], cells[at, 128:256]
        swapped = pltpu.roll(pair, 64, 1)
        each = (jnp.where(left, pair, swapped), jnp.where(left, swapped, pair), jnp.where(left, third, pltpu.roll(third, 64, 1)))
        lhs = jnp.concatenate(
            [jnp.where(ownpart, jnp.concatenate([e] * 4, axis=1), 0.0) for e in each], axis=0
        ).astype(BF16)
        result = 20.0 * dot(lhs, weights[512 * g : 512 * g + 512, :])
        for k in range(3):
            part = result[8 * k : 8 * k + 8]
            speed[k, at, :] = part
            means[k].append(jnp.sum(part, axis=1, keepdims=True) * (1.0 / 128.0))
    stores[1].start()
    belongs = member[...]
    swim[...] = jnp.concatenate(
        [jnp.sum(jnp.concatenate(means[k], axis=0) * belongs, axis=0, keepdims=True) for k in range(3)], axis=0
    )
    stores[2].start()
    for store in stores:
        store.wait()


def body(populations, marker_weights, marker_force, owner_device, stencil_base, block_swimmer):
    vmem = pl.BlockSpec(memory_space=pltpu.VMEM)
    hbm = pl.BlockSpec(memory_space=pl.ANY)
    operands = (
        populations,
        marker_weights.reshape(HELD * 64, 128),
        marker_force.transpose(1, 0, 2),
        owner_device.reshape(1, HELD),
        stencil_base.T,
        block_swimmer.reshape(1, HELD),
    )
    handed = pl.pallas_call(
        kernel,
        out_shape=(
            jax.ShapeDtypeStruct((19, CX, CY, NZ), F32),
            jax.ShapeDtypeStruct((NDEV, 4, 128), F32),
            jax.ShapeDtypeStruct((HELD * 64, 128), BF16),
            jax.ShapeDtypeStruct((HELD, 256), BF16),
            jax.ShapeDtypeStruct((HELD, 4), F32),
        ),
        in_specs=[hbm] * 6,
        out_specs=(vmem,) * 5,
        scratch_shapes=[
            pltpu.VMEM((19, CX, CY, NZ), F32),
            pltpu.VMEM((3, HELD, 128), BF16),
            pltpu.VMEM((1, HELD), jnp.int32),
            pltpu.VMEM((3, HELD), jnp.int32),
            pltpu.VMEM((1, HELD), jnp.int32),
            pltpu.VMEM((NDEV, 4, 128), F32),
            pltpu.VMEM((NDEV, 4, 128), F32),
            pltpu.VMEM((NDEV, 4, 128), F32),
            pltpu.VMEM((2, 256, 128), F32),
            pltpu.VMEM((3, 256, 1024), BF16),
            pltpu.VMEM((1024, 128), BF16),
            pltpu.VMEM((3, CX, CY, NZ), F32),
            pltpu.VMEM((19, CX + 2, CY + 16, NZ), F32),
            pltpu.VMEM((19, CX + 2, CY + 16, NZ), F32),
            pltpu.VMEM((3, CX, CY, NZ), F32),
            pltpu.VMEM((384, 1024), F32),
            pltpu.VMEM((2, 256, 128), F32),
            pltpu.VMEM((2, 2, 5, 4, 128), F32),
            pltpu.VMEM((2, 2, 5, 4, 128), F32),
            pltpu.VMEM((2, 4, 1, 128), F32),
            pltpu.VMEM((2, 4, 1, 128), F32),
            pltpu.SemaphoreType.DMA((6,)),
            pltpu.SemaphoreType.DMA((2,)),
            pltpu.SemaphoreType.DMA((2,)),
            pltpu.SemaphoreType.DMA((2, 8)),
            pltpu.SemaphoreType.DMA((2, 8)),
        ],
        compiler_params=pltpu.CompilerParams(
            collective_id=0, has_side_effects=True, vmem_limit_bytes=40 * 1024 * 1024
        ),
    )(
        *(pltpu.with_memory_space_constraint(x, pltpu.HBM) for x in operands)
    )
    fields, speed, swim = pl.pallas_call(
        finish,
        out_shape=(
            jax.ShapeDtypeStruct((19, CX, CY, NZ), F32),
            jax.ShapeDtypeStruct((3, HELD, 128), F32),
            jax.ShapeDtypeStruct((3, 4), F32),
        ),
        in_specs=[vmem] * 5,
        out_specs=(hbm,) * 3,
        scratch_shapes=[
            pltpu.VMEM((3, HELD, 128), F32),
            pltpu.VMEM((3, 4), F32),
            pltpu.SemaphoreType.DMA((3,)),
        ],
        compiler_params=pltpu.CompilerParams(vmem_limit_bytes=16 * 1024 * 1024),
    )(*handed)
    return fields, speed.transpose(1, 0, 2), swim


def solution(mesh):
    in_specs = (
        P(None, "gx", "gy", None),
        P(("gx", "gy"), None, None),
        P(("gx", "gy"), None, None),
        P(("gx", "gy"), None),
        P(("gx", "gy"), None),
        P(("gx", "gy")),
    )
    out_specs = (P(None, "gx", "gy", None), P(("gx", "gy"), None, None), P(None, ("gx", "gy")))
    return jax.shard_map(body, mesh=mesh, in_specs=in_specs, out_specs=out_specs, check_vma=False)
```

```python
import jax
import jax.numpy as jnp
from jax import lax
from jax.experimental import pallas as pl
from jax.experimental.pallas import tpu as pltpu
from jax.sharding import PartitionSpec as P

MESH = pl.DeviceIdType.MESH
F32 = jnp.float32
BF16 = jnp.bfloat16

NGX, NGY, NDEV = 16, 8, 128
CX, CY, NZ = 4, 32, 128
HELD = 48
TOP = 8

VEL = (
    (0, 0, 0),
    (1, 0, 0), (-1, 0, 0), (0, 1, 0), (0, -1, 0), (0, 0, 1), (0, 0, -1),
    (1, 1, 0), (-1, -1, 0), (1, -1, 0), (-1, 1, 0),
    (1, 0, 1), (-1, 0, -1), (1, 0, -1), (-1, 0, 1),
    (0, 1, 1), (0, -1, -1), (0, 1, -1), (0, -1, 1),
)
OPP = (0, 2, 1, 4, 3, 6, 5, 8, 7, 10, 9, 12, 11, 14, 13, 16, 15, 18, 17)
WEIGHT = (1.0 / 3.0,) + (1.0 / 18.0,) * 6 + (1.0 / 36.0,) * 12
PAIRS = ((1, 2), (3, 4), (5, 6), (7, 8), (9, 10), (11, 12), (13, 14), (15, 16), (17, 18))

XP = (1, 7, 9, 11, 13)
XM = (2, 8, 10, 12, 14)
REST = (0, 3, 4, 5, 6, 15, 16, 17, 18)
ORDER = XP + XM + REST
AT = {d: i for i, d in enumerate(ORDER)}
YP = (3, 7, 10, 15, 17)
YM = (4, 8, 9, 16, 18)


def iota(shape, dim):
    return lax.broadcasted_iota(jnp.int32, shape, dim)


def dot(a, b):
    return jnp.dot(a, b, preferred_element_type=F32)


def dot_nt(a, b):
    return lax.dot_general(a, b, (((1,), (1,)), ((), ())), preferred_element_type=F32)


def own_part():
    return lax.div(iota((8, 512), 1), 64) == iota((8, 512), 0)


def moments(f):
    rho = f[0]
    mom = [None, None, None]
    for p, m in PAIRS:
        rho = rho + (f[p] + f[m])
        diff = f[p] - f[m]
        for k in range(3):
            if VEL[p][k] == 1:
                mom[k] = diff if mom[k] is None else mom[k] + diff
            elif VEL[p][k] == -1:
                mom[k] = mom[k] - diff
    return rho, mom


def collide(f, force):
    rho, mom = moments(f)
    inv = 1.0 / rho
    u = [(mom[k] + 0.8 * force[k]) * inv for k in range(3)]
    usq = u[0] * u[0] + u[1] * u[1] + u[2] * u[2]
    whole = 1.25 * rho
    calm = 1.0 - 1.5 * usq
    out = [None] * 19
    out[0] = (WEIGHT[0] * whole) * calm - 0.25 * f[0]
    for first, last, w in ((0, 3, 1.0 / 18.0), (3, 9, 1.0 / 36.0)):
        scaled = w * whole
        base = scaled * calm
        linear = 3.0 * scaled
        for p, m in PAIRS[first:last]:
            along = None
            for k in range(3):
                if VEL[p][k] == 1:
                    along = u[k] if along is None else along + u[k]
                elif VEL[p][k] == -1:
                    along = along - u[k]
            turn = linear * along
            even = base + 1.5 * (turn * along)
            out[p] = (even + turn) - 0.25 * f[p]
            out[m] = (even - turn) - 0.25 * f[m]
    return out


def kernel(
    pop_hbm, weights_hbm, force_hbm, owner_hbm, base_hbm, swimmer_hbm,
    new_pop, finbuf, weights, take_out, member_out,
    pop, force, owner, base, swimmer,
    sendbuf, recvbuf, backbuf, turned, spread, onehot_z, forcing, pad1, pad2, fluid, sampled, samples,
    ysend, yrecv, csend, crecv,
    load_sem, send_sem, recv_sem, halo_send, halo_recv,
):
    loads = [
        pltpu.make_async_copy(source, target, load_sem.at[i])
        for i, (source, target) in enumerate(
            ((owner_hbm, owner), (base_hbm, base), (force_hbm, force), (weights_hbm, weights), (swimmer_hbm, swimmer), (pop_hbm, pop))
        )
    ]
    gx, gy = lax.axis_index("gx"), lax.axis_index("gy")
    me = gx * NGY + gy
    core, my_x = lax.rem(gx, 2), lax.rem(lax.div(gx, 2), 4)
    my_y, my_z = lax.div(gy, 2), lax.div(gx, 8) * 2 + lax.rem(gy, 2)

    along_x = [lax.rem(my_x + d, 4) * 2 for d in (1, 3, 2, 0)]

    def to_all(act):
        def offset(digit):
            return jnp.where(digit < 2, 2 - digit, lax.rem(digit + 1, 4))

        def step(i, _):
            z = lax.rem(my_z + offset(lax.div(i, 4)), 4)
            tx = lax.div(z, 2) * 8
            ty = lax.rem(my_y + offset(lax.rem(i, 4)), 4) * 2 + lax.rem(z, 2)
            for x in along_x:
                act(tx + x, ty)
                act(tx + x + 1, ty)
            return 0

        lax.fori_loop(0, 15, step, 0)
        first = lax.div(gx, 8) * 8
        for x in along_x[:3]:
            act(first + x, gy)
            act(first + x + 1, gy)
        act(gx + 1 - 2 * core, gy)

    barrier = pltpu.get_barrier_semaphore()
    to_all(lambda tx, ty: pl.semaphore_signal(barrier, inc=1, device_id=(tx, ty), device_id_type=MESH))

    for load in loads:
        load.start()

    for load in loads[:4]:
        load.wait()
    square = (HELD, HELD)
    down, across = iota(square, 0), iota(square, 1)

    def standing(line):
        return jnp.sum(jnp.where(down == across, line, 0), axis=1, keepdims=True)

    row = owner[...]
    col = standing(row)
    same = col == row
    rank_col = jnp.sum(jnp.where(same & (across < down), 1, 0), axis=1, keepdims=True)
    rank_row = jnp.sum(jnp.where(same & (down < across), 1, 0), axis=0, keepdims=True)
    slot_row = rank_row * NDEV + row
    slot_col = rank_col * NDEV + col

    take_out[...] = jnp.where(iota((HELD, 256), 1) == slot_col, 1.0, 0.0).astype(BF16)
    loads[4].wait()
    member_out[...] = jnp.where(lax.rem(standing(swimmer[...]), 4) == iota((HELD, 4), 1), 1.0, 0.0)

    lane = iota((8, 128), 1)
    left = lane < 64
    ownpart = own_part()
    pulls = [force[k].astype(F32) for k in range(3)]
    strip = standing(base[1:2, :]).astype(F32)
    column = standing(base[2:3, :]).astype(F32)
    rows01, rows2x = [], []
    for g in range(6):
        at = slice(8 * g, 8 * g + 8)
        lhs = jnp.concatenate([pulls[k][at] for k in range(3)], axis=0).astype(BF16)
        full = dot_nt(lhs, weights[512 * g : 512 * g + 512, :])
        part = []
        for k in range(3):
            x = jnp.where(ownpart, full[8 * k : 8 * k + 8], 0.0)
            y = (x[:, 0:128] + x[:, 128:256]) + (x[:, 256:384] + x[:, 384:512])
            part.append(y + pltpu.roll(y, 64, 1))
        extra = jnp.where(lane == 64, strip[at], jnp.where(lane == 65, column[at], 0.0))
        rows01.append(jnp.where(left, part[0], part[1]))
        rows2x.append(jnp.where(left, part[2], extra))
    patch = jnp.concatenate([jnp.concatenate(rows01, axis=0), jnp.concatenate(rows2x, axis=0)], axis=1)
    patch_hi = patch.astype(BF16)
    patch_lo = (patch - patch_hi.astype(F32)).astype(BF16)
    put = jnp.where(iota((256, HELD), 0) == slot_row, 1.0, 0.0).astype(BF16)
    outgoing = dot(put, patch_hi) + dot(put, patch_lo)
    for j in range(2):
        for h in range(2):
            sendbuf[:, 2 * j + h, :] = outgoing[128 * j : 128 * j + 128, 128 * h : 128 * h + 128]

    pl.semaphore_wait(barrier, NDEV - 1)

    def exchange(source, target, n, rows=4):
        to_all(
            lambda tx, ty: pltpu.make_async_remote_copy(
                source.at[tx * NGY + ty, 0:rows], target.at[me, 0:rows], send_sem.at[n], recv_sem.at[n],
                device_id=(tx, ty), device_id_type=MESH,
            ).start()
        )
        target[me, 0:rows] = source[me, 0:rows]

    def exchanged(source, target, n, rows=4):
        return pltpu.make_async_remote_copy(
            source.at[pl.ds(0, NDEV - 1), 0:rows], target.at[pl.ds(0, NDEV - 1), 0:rows], send_sem.at[n], recv_sem.at[n],
            device_id=(lax.rem(gx + 1, NGX), gy), device_id_type=MESH,
        )

    exchange(sendbuf, recvbuf, 0)
    exchanged(sendbuf, recvbuf, 0).wait_recv()

    wide = iota((128, 128), 1)
    for j in range(2):
        for h in range(2):
            got = recvbuf[:, 2 * j + h, :]
            turned[j, 128 * h : 128 * h + 128, :] = got.T
            if h == 1:
                ahead = wide - jnp.broadcast_to(got[:, 65:66], (128, 128)).astype(jnp.int32)
                for c in range(4):
                    onehot_z[256 * c + 128 * j : 256 * c + 128 * j + 128, :] = jnp.where(
                        ahead == c, 1.0, 0.0
                    ).astype(BF16)
    sub = iota((8, 128), 0)
    bits, inside = [], []
    for j in range(2):
        y_first = jnp.broadcast_to(turned[j, 192:193, :].astype(jnp.int32), (8, 128))
        bits.append([(y_first & n) != 0 for n in (1, 2, 4)])
        offs = [sub + 8 * v - y_first for v in range(4)]
        inside.append([(off >= 0) & (off < 4) for off in offs])

    def place(k, a):
        ka = CX * k + a
        for c in range(4):
            for j in range(2):
                x = turned[j, pl.ds(ka * 16 + c, 8, stride=4), :]
                for n, bit in zip((1, 2, 4), bits[j]):
                    x = jnp.where(bit, pltpu.roll(x, n, 0), x)
                hi = x.astype(BF16).astype(F32)
                lo = x - hi
                start = 256 * c + 128 * j
                for piece, rows in ((hi, slice(32 * a, 32 * a + 32)), (lo, slice(128 + 32 * a, 160 + 32 * a))):
                    spread[k, rows, start : start + 128] = jnp.concatenate(
                        [jnp.where(inside[j][v], piece, 0.0) for v in range(4)], axis=0
                    ).astype(BF16)

    for k in range(3):
        for a in range(CX):
            place(k, a)
        both = dot(spread[k], onehot_z[...])
        forcing[k] = (both[:128] + both[128:]).reshape(CX, CY, NZ)

    east, west = (lax.rem(gx + 1, NGX), gy), (lax.rem(gx + NGX - 1, NGX), gy)
    up, down_ = lax.rem(gy + 1, NGY), lax.rem(gy + NGY - 1, NGY)
    north, south = (gx, up), (gx, down_)
    corners = ((7, (east[0], up)), (8, (west[0], down_)), (9, (east[0], down_)), (10, (west[0], up)))

    zlane = iota((8, NZ), 1)
    ysub = iota((8, NZ), 0)
    at_low, at_high = gy == 0, gy == NGY - 1

    def pulled(pad, d, x, yc):
        ex, ey, ez = VEL[d]
        value = pad[AT[d], x + 1 - ex, TOP + 8 * yc - ey : TOP + 8 * yc - ey + 8, :]
        wall = []
        if ez:
            value = pltpu.roll(value, 1 if ez == 1 else NZ - 1, 1)
            wall.append(zlane == (0 if ez == 1 else NZ - 1))
        if ey == 1 and yc == 0:
            wall.append((ysub == 0) & at_low)
        if ey == -1 and yc == 3:
            wall.append((ysub == 7) & at_high)
        if wall:
            mask = wall[0] if len(wall) == 1 else wall[0] | wall[1]
            value = jnp.where(mask, pad[AT[OPP[d]], x + 1, TOP + 8 * yc : TOP + 8 * yc + 8, :], value)
        return value

    def collided(pad, f, x, yc):
        at = slice(8 * yc, 8 * yc + 8)
        out = collide(f, [forcing[k, x, at, :] for k in range(3)])
        for d in range(19):
            pad[AT[d], x + 1, TOP + 8 * yc : TOP + 8 * yc + 8, :] = out[d]

    def halo_copy(source, target, n, i, device):
        c = pltpu.make_async_remote_copy(
            source, target, halo_send.at[n, i], halo_recv.at[n, i], device_id=device, device_id_type=MESH
        )
        c.start()
        return c

    def send_corners(pad, n):
        copies = []
        for i, (d, device) in enumerate(corners):
            x = CX if VEL[d][0] == 1 else 1
            y = TOP + CY - 1 if VEL[d][1] == 1 else TOP
            csend[n, i] = pad[AT[d], x, y : y + 1, :]
            copies.append(halo_copy(csend.at[n, i], crecv.at[n, i], n, 4 + i, device))
        return copies

    def send_x(pad, n):
        rows = pl.ds(TOP, CY)
        return [
            halo_copy(pad.at[0:5, CX, rows, :], pad.at[0:5, 0, rows, :], n, 0, east),
            halo_copy(pad.at[5:10, 1, rows, :], pad.at[5:10, CX + 1, rows, :], n, 1, west),
        ]

    def send_y(pad, n):
        copies = []
        for side, dirs, edge, device in ((0, YP, TOP + CY - 1, north), (1, YM, TOP, south)):
            for i, d in enumerate(dirs):
                for x in range(CX):
                    ysend[n, side, i, x : x + 1, :] = pad[AT[d], x + 1, edge : edge + 1, :]
            copies.append(halo_copy(ysend.at[n, side], yrecv.at[n, side], n, 2 + side, device))
        return copies

    def halo_finish(pad, n, copies):
        for c in copies:
            c.wait_recv()
        for side, dirs, edge in ((0, YP, TOP - 1), (1, YM, TOP + CY)):
            for i, d in enumerate(dirs):
                for x in range(CX):
                    pad[AT[d], x + 1, edge : edge + 1, :] = yrecv[n, side, i, x : x + 1, :]
        for i, (d, device) in enumerate(corners):
            x = 0 if VEL[d][0] == 1 else CX + 1
            y = TOP - 1 if VEL[d][1] == 1 else TOP + CY
            pad[AT[d], x, y : y + 1, :] = crecv[n, i]

    def cells(work, xs, ycs):
        for x in xs:
            for yc in ycs:
                work(x, yc)

    outer, inner = (0, 3), (1, 2)

    def rim_sent(work, pad, n):
        cells(work, outer, outer)
        copies = send_corners(pad, n)
        cells(work, outer, inner)
        copies += send_x(pad, n)
        cells(work, inner, outer)
        return copies + send_y(pad, n)

    def step1(x, yc):
        collided(pad1, [pop[d, x, 8 * yc : 8 * yc + 8, :] for d in range(19)], x, yc)

    def step2(x, yc):
        collided(pad2, [pulled(pad1, d, x, yc) for d in range(19)], x, yc)

    def step3(x, yc):
        at = slice(8 * yc, 8 * yc + 8)
        rho, mom = moments([pulled(pad2, d, x, yc) for d in range(19)])
        inv = 1.0 / rho
        for k in range(3):
            fluid[k, x, at, :] = (mom[k] + 0.5 * forcing[k, x, at, :]) * inv

    def keep(x, yc):
        for d in range(19):
            new_pop[d, x, 8 * yc : 8 * yc + 8, :] = pulled(pad2, d, x, yc)

    every = range(4)
    loads[5].wait()
    halo1 = rim_sent(step1, pad1, 0)
    cells(step1, inner, inner)
    cells(step2, inner, inner)
    halo_finish(pad1, 0, halo1)
    halo2 = rim_sent(step2, pad2, 1)
    cells(step3, inner, inner)
    halo_finish(pad2, 1, halo2)
    cells(step3, outer, every)
    cells(step3, inner, outer)

    def sample(ka):
        for c in range(4):
            for j in range(2):
                cols = slice(256 * c + 128 * j, 256 * c + 128 * j + 128)
                x = sampled[slice(32 * ka, 32 * ka + 8), cols]
                for v in range(1, 4):
                    x = jnp.where(inside[j][v], sampled[slice(32 * ka + 8 * v, 32 * ka + 8 * v + 8), cols], x)
                for n, bit in zip((1, 2, 4), bits[j]):
                    x = jnp.where(bit, pltpu.roll(x, 8 - n, 0), x)
                samples[j, pl.ds(ka * 16 + c, 4, stride=4), :] = x[0:4]

    for k in range(3):
        sampled[128 * k : 128 * k + 128, :] = dot_nt(fluid[k].reshape(128, NZ).astype(BF16), onehot_z[...])
        for a in range(CX):
            sample(CX * k + a)
    for j in range(2):
        backbuf[:, j, :] = samples[j, 0:128, :].T
    backbuf[:, 2, :] = jnp.concatenate([samples[j, 128:192, :] for j in range(2)], axis=0).T
    exchange(backbuf, finbuf, 1, 3)
    lax.fori_loop(0, CX, lambda x, c: (cells(keep, (x,), every), c)[1], 0)
    exchanged(backbuf, finbuf, 1, 3).wait_recv()

    exchanged(sendbuf, recvbuf, 0).wait_send()
    exchanged(backbuf, finbuf, 1, 3).wait_send()
    for c in halo1 + halo2:
        c.wait_send()


def finish(
    fields, finbuf, weights, take, member,
    fields_hbm, speed_hbm, swim_hbm,
    speed, swim, sem,
):
    stores = [
        pltpu.make_async_copy(source, target, sem.at[i])
        for i, (source, target) in enumerate(((fields, fields_hbm), (speed, speed_hbm), (swim, swim_hbm)))
    ]
    stores[0].start()
    left = iota((8, 128), 1) < 64
    ownpart = own_part()
    thirds = finbuf[:, 2, :]
    back = jnp.concatenate(
        [
            jnp.concatenate([finbuf[:, 0, :], thirds], axis=1),
            jnp.concatenate([finbuf[:, 1, :], pltpu.roll(thirds, 64, 1)], axis=1),
        ],
        axis=0,
    ).astype(BF16)
    cells = dot(take[...], back)
    means = [[], [], []]
    for g in range(6):
        at = slice(8 * g, 8 * g + 8)
        pair, third = cells[at, 0:128], cells[at, 128:256]
        swapped = pltpu.roll(pair, 64, 1)
        each = (jnp.where(left, pair, swapped), jnp.where(left, swapped, pair), jnp.where(left, third, pltpu.roll(third, 64, 1)))
        lhs = jnp.concatenate(
            [jnp.where(ownpart, jnp.concatenate([e] * 4, axis=1), 0.0) for e in each], axis=0
        ).astype(BF16)
        result = 20.0 * dot(lhs, weights[512 * g : 512 * g + 512, :])
        for k in range(3):
            part = result[8 * k : 8 * k + 8]
            speed[k, at, :] = part
            means[k].append(jnp.sum(part, axis=1, keepdims=True) * (1.0 / 128.0))
    stores[1].start()
    belongs = member[...]
    swim[...] = jnp.concatenate(
        [jnp.sum(jnp.concatenate(means[k], axis=0) * belongs, axis=0, keepdims=True) for k in range(3)], axis=0
    )
    stores[2].start()
    for store in stores:
        store.wait()


def body(populations, marker_weights, marker_force, owner_device, stencil_base, block_swimmer):
    vmem = pl.BlockSpec(memory_space=pltpu.VMEM)
    hbm = pl.BlockSpec(memory_space=pl.ANY)
    operands = (
        populations,
        marker_weights.reshape(HELD * 64, 128),
        marker_force.transpose(1, 0, 2),
        owner_device.reshape(1, HELD),
        stencil_base.T,
        block_swimmer.reshape(1, HELD),
    )
    handed = pl.pallas_call(
        kernel,
        out_shape=(
            jax.ShapeDtypeStruct((19, CX, CY, NZ), F32),
            jax.ShapeDtypeStruct((NDEV, 4, 128), F32),
            jax.ShapeDtypeStruct((HELD * 64, 128), BF16),
            jax.ShapeDtypeStruct((HELD, 256), BF16),
            jax.ShapeDtypeStruct((HELD, 4), F32),
        ),
        in_specs=[hbm] * 6,
        out_specs=(vmem,) * 5,
        scratch_shapes=[
            pltpu.VMEM((19, CX, CY, NZ), F32),
            pltpu.VMEM((3, HELD, 128), BF16),
            pltpu.VMEM((1, HELD), jnp.int32),
            pltpu.VMEM((3, HELD), jnp.int32),
            pltpu.VMEM((1, HELD), jnp.int32),
            pltpu.VMEM((NDEV, 4, 128), F32),
            pltpu.VMEM((NDEV, 4, 128), F32),
            pltpu.VMEM((NDEV, 4, 128), F32),
            pltpu.VMEM((2, 256, 128), F32),
            pltpu.VMEM((3, 256, 1024), BF16),
            pltpu.VMEM((1024, 128), BF16),
            pltpu.VMEM((3, CX, CY, NZ), F32),
            pltpu.VMEM((19, CX + 2, CY + 16, NZ), F32),
            pltpu.VMEM((19, CX + 2, CY + 16, NZ), F32),
            pltpu.VMEM((3, CX, CY, NZ), F32),
            pltpu.VMEM((384, 1024), F32),
            pltpu.VMEM((2, 256, 128), F32),
            pltpu.VMEM((2, 2, 5, 4, 128), F32),
            pltpu.VMEM((2, 2, 5, 4, 128), F32),
            pltpu.VMEM((2, 4, 1, 128), F32),
            pltpu.VMEM((2, 4, 1, 128), F32),
            pltpu.SemaphoreType.DMA((6,)),
            pltpu.SemaphoreType.DMA((2,)),
            pltpu.SemaphoreType.DMA((2,)),
            pltpu.SemaphoreType.DMA((2, 8)),
            pltpu.SemaphoreType.DMA((2, 8)),
        ],
        compiler_params=pltpu.CompilerParams(
            collective_id=0, has_side_effects=True, vmem_limit_bytes=40 * 1024 * 1024
        ),
    )(
        *(pltpu.with_memory_space_constraint(x, pltpu.HBM) for x in operands)
    )
    fields, speed, swim = pl.pallas_call(
        finish,
        out_shape=(
            jax.ShapeDtypeStruct((19, CX, CY, NZ), F32),
            jax.ShapeDtypeStruct((3, HELD, 128), F32),
            jax.ShapeDtypeStruct((3, 4), F32),
        ),
        in_specs=[vmem] * 5,
        out_specs=(hbm,) * 3,
        scratch_shapes=[
            pltpu.VMEM((3, HELD, 128), F32),
            pltpu.VMEM((3, 4), F32),
            pltpu.SemaphoreType.DMA((3,)),
        ],
        compiler_params=pltpu.CompilerParams(vmem_limit_bytes=16 * 1024 * 1024),
    )(*handed)
    return fields, speed.transpose(1, 0, 2), swim


def solution(mesh):
    in_specs = (
        P(None, "gx", "gy", None),
        P(("gx", "gy"), None, None),
        P(("gx", "gy"), None, None),
        P(("gx", "gy"), None),
        P(("gx", "gy"), None),
        P(("gx", "gy")),
    )
    out_specs = (P(None, "gx", "gy", None), P(("gx", "gy"), None, None), P(None, ("gx", "gy")))
    return jax.shard_map(body, mesh=mesh, in_specs=in_specs, out_specs=out_specs, check_vma=False)
```
